32 devices in a mesh: tm: 16 (over z, y, x), blk: 2 (over core).
Axes of the slice: x: 2, y: 2, z: 4, core: 2. Of those that a mesh axis runs over, the one named last changes fastest.
Arguments:
- diag_block: float32 [32, 1024, 1024], P('tm', 'blk'), may hold values from -24.5 to 25.25, as said below
- coupling: float32 [32, 1024, 1024], P('tm', 'blk'), may hold values from -12.25 to 12.25
- arrow: float32 [32, 64, 1024], P('tm', 'blk'), may hold values from -0.25 to 0.25
- corner: float32 [64, 64], P('blk'), may hold values from -6 to 6
Outputs:
- inner_pivot: float32 [16, 1024, 1024], P('tm', 'blk')
- inner_left: float32 [16, 1024, 1024], P('tm', 'blk')
- inner_right: float32 [16, 1024, 1024], P('tm', 'blk')
- inner_arrow: float32 [16, 64, 1024], P('tm', 'blk')
- pivot: float32 [16, 1024, 1024], P('tm', 'blk')
- left_factor_even: float32 [16, 1024, 1024], P('tm', 'blk')
- right_factor_even: float32 [16, 1024, 1024], P('tm', 'blk')
- arrow_factor_even: float32 [16, 64, 1024], P('tm', 'blk')
- corner_out: float32 [64, 64], P('blk')
The draws below stay inside these ranges and needn't reach their ends.
Inputs may be any that keep to these rules, and one draw needn't show every extreme that they name: `diag_block`: Symmetric; together with the coupling blocks the matrix of all day blocks is positive definite.
All inputs are finite; a program needn't handle non-finite values.
Results may differ from the reference program's by a relative error of at most 0.00014.
Values sent between devices are 32-bit elements; how exact they have to be, the bound alone decides.
No kernel may reach another device: no remote copies, remote signals or barrier semaphores. Data moves between devices by JAX's collectives and lax.ppermute only.
A program may use at most 128 MiB of HBM per device.

```python
import jax
import jax.numpy as jnp
from jax import lax

NODES = 1024
EFFECTS = 64
DAYS = 32
N_TM = 16


def factor_rows(key, day, value_salt, scale_salt, scale_top):
    value_key = jax.random.fold_in(jax.random.fold_in(key, value_salt), day)
    scale_key = jax.random.fold_in(jax.random.fold_in(key, scale_salt), day)
    values = jax.random.randint(value_key, (NODES, NODES), -7, 8).astype(jnp.float32)
    scales = jax.random.randint(scale_key, (NODES,), 1, scale_top + 1).astype(jnp.float32)
    return values * scales[:, None]


def outer_rows(left, right):
    return lax.dot_general(left, right, (((1,), (1,)), ((), ())), precision=lax.Precision.HIGHEST, preferred_element_type=jnp.float32)


def coupling_blocks(key, scale_top, step):

    def one_day(day):
        own_rows = factor_rows(key, day, 21, 22, scale_top)
        next_rows = factor_rows(key, day, 23, 24, scale_top)
        return outer_rows(next_rows, own_rows) * step
    return lax.map(one_day, jnp.arange(DAYS, dtype=jnp.int32))


def diagonal_blocks(key, scale_top, step, shift):

    def one_day(inputs):
        day, shift_row = inputs
        own_rows = factor_rows(key, day, 21, 22, scale_top)
        earlier = jnp.maximum(day - 1, 0)
        back_rows = factor_rows(key, earlier, 23, 24, scale_top) * (day > 0).astype(jnp.float32)
        summed = outer_rows(own_rows, own_rows) + outer_rows(back_rows, back_rows)
        identity = jnp.eye(NODES, dtype=jnp.float32)
        return summed * step + shift_row[:, None] * identity
    return lax.map(one_day, (jnp.arange(DAYS, dtype=jnp.int32), shift))


def draw_coupling(key, part):
    blocks = coupling_blocks(key, 1, 2.0 ** (-14))
    return blocks


def draw_diag_block(key, part):
    shift_key = jax.random.fold_in(key, 5)
    shift = jax.random.randint(shift_key, (DAYS, NODES), 32, 97).astype(jnp.float32) * 2.0 ** (-7)
    blocks = diagonal_blocks(key, 1, 2.0 ** (-14), shift)
    return blocks


def level_of(stream_key, dims, split, least, largest):
    gain = 1.0
    for axis_at, blocks in split:
        draws = jax.random.uniform(jax.random.fold_in(jax.random.fold_in(stream_key, 6), axis_at), (blocks,), jnp.float32, least / len(split), largest / len(split))
        gain = gain * jnp.repeat(jnp.exp(draws), dims[axis_at] // blocks).reshape((-1,) + (1,) * (len(dims) - 1 - axis_at))
    return gain


def gaussian(rng, shape, spread, most, cuts=(), kind=jnp.bfloat16):
    gain = level_of(rng, shape, cuts, -0.22, 0.18) if cuts else 1.0
    result = jax.random.normal(rng, shape, jnp.float32) * spread * gain
    return jnp.minimum(jnp.maximum(result, -most), most).astype(kind)


def setup_inputs(seed: int = 0) -> dict:
    arg_keys = jax.random.split(jax.random.key(seed), 5)
    diag_block = draw_diag_block(jax.random.fold_in(arg_keys[4], 71), 0)
    coupling = draw_coupling(jax.random.fold_in(arg_keys[4], 71), 0)
    arrow = gaussian(arg_keys[2], (DAYS, EFFECTS, NODES), (DAYS * NODES // 64) ** -0.5, 0.25, ((0, 16), (1, 2)), jnp.float32)
    corner = gaussian(arg_keys[3], (EFFECTS, EFFECTS), 1.0, 6.0, ((0, 2),), jnp.float32)
    return dict(diag_block=diag_block, coupling=coupling, arrow=arrow, corner=corner)


def transposed_product(left, right):
    return lax.dot_general(left.astype(jnp.float32), right.astype(jnp.float32), (((0,), (0,)), ((), ())), precision=lax.Precision.HIGHEST, preferred_element_type=jnp.float32)

def factor_solve(pivot_rows, right_hand):
    factor = jnp.linalg.cholesky(pivot_rows)
    solved = jax.scipy.linalg.solve_triangular(factor, right_hand, lower=True)
    return (factor, solved)

def split_product(solved, node_count):
    product = transposed_product(solved, solved)
    first_first = product[:node_count, :node_count]
    second_second = product[node_count:2 * node_count, node_count:2 * node_count]
    second_first = product[node_count:2 * node_count, :node_count]
    arrow_first = product[2 * node_count:, :node_count]
    arrow_second = product[2 * node_count:, node_count:2 * node_count]
    arrow_arrow = product[2 * node_count:, 2 * node_count:]
    return (first_first, second_second, second_first, arrow_first, arrow_second, arrow_arrow)

def reference(diag_block, coupling, arrow, corner):
    partition_count = N_TM
    node_count = NODES
    open_end = (jnp.arange(partition_count) < partition_count - 1).astype(jnp.float32)

    def interior(slab_index):
        interior_day = 2 * slab_index + 1
        pivot_rows = lax.dynamic_index_in_dim(diag_block, interior_day, 0, False)
        backward = lax.dynamic_index_in_dim(coupling, 2 * slab_index, 0, False)
        forward = lax.dynamic_index_in_dim(coupling, interior_day, 0, False) * lax.dynamic_index_in_dim(open_end, slab_index, 0, False)
        arrow_part = lax.dynamic_index_in_dim(arrow, interior_day, 0, False)
        factor, solved = factor_solve(pivot_rows, jnp.concatenate([backward, forward.T, arrow_part.T], axis=1))
        blocks = split_product(solved, node_count)
        return (factor, solved[:, :node_count].T, solved[:, node_count:2 * node_count].T, solved[:, 2 * node_count:].T) + blocks
    results = lax.map(interior, jnp.arange(partition_count, dtype=jnp.int32))
    inner_pivot, inner_left, inner_right, inner_arrow = (results[0], results[1], results[2], results[3])
    first_first, second_second, second_first, arrow_first, arrow_second, arrow_arrow = results[4:]

    def shift_down(values):
        return jnp.concatenate([jnp.zeros_like(values[:1]), values[:-1]], axis=0)
    pivot = diag_block[0::2] - first_first - shift_down(second_second)
    right_coupling_block = -second_first
    arrow_factor_even = arrow[0::2] - arrow_first - shift_down(arrow_second)
    left_factor_even = shift_down(jnp.swapaxes(right_coupling_block, 1, 2))
    corner_out = corner - jnp.sum(arrow_arrow, axis=0)
    return (inner_pivot, inner_left, inner_right, inner_arrow, pivot, left_factor_even, right_coupling_block, arrow_factor_even, corner_out)
```

```python
import functools

import jax
import jax.numpy as jnp
from jax import lax
from jax.experimental import pallas as pl
from jax.experimental.pallas import tpu as pltpu
from jax.sharding import PartitionSpec as P

BLOCK = 128
PANEL = 256
SMALL = pl.CostEstimate(flops=10**6, bytes_accessed=10**4, transcendentals=0)


def shifted(value, axis, steps):
    count = lax.axis_size(axis)
    leading, last = (max(0, -steps), min(count, count - steps))
    return lax.ppermute(value, axis, [(source, source + steps) for source in range(leading, last)])


def swapped(value):
    return lax.ppermute(value, "blk", [(0, 1), (1, 0)])


def after(value, *earlier):
    return lax.optimization_barrier((value, *earlier))[0]


def paired_sum(value, axis, steps, *earlier):
    count = lax.axis_size(axis)
    received = lax.ppermute(value, axis, [(source, source ^ steps) for source in range(count)])
    return value + after(received, *earlier)


def exact(left, right, right_dim):
    return lax.dot_general(
        left, right, (((1,), (right_dim,)), ((), ())), precision=lax.Precision.HIGHEST, preferred_element_type=jnp.float32
    )


def plain_nt(left, right):
    return lax.dot_general(left, right, (((1,), (1,)), ((), ())), preferred_element_type=jnp.float32)


def split(value):
    high = value.astype(jnp.bfloat16)
    low = (value - high.astype(jnp.float32)).astype(jnp.bfloat16)
    return high, low


def left_terms(high, low):
    return jnp.concatenate([high, low, high], axis=1)


def right_terms(high, low):
    return jnp.concatenate([high, high, low], axis=1)


def inverse_of_factor(block, tasks):
    shape = (8, BLOCK)
    lane = lax.broadcasted_iota(jnp.int32, shape, 1)
    sub = lax.broadcasted_iota(jnp.int32, shape, 0)

    def along_lanes(value, at):
        return jnp.broadcast_to(value[:, at : at + 1], shape)

    def along_rows(value, at):
        return jnp.broadcast_to(value[at : at + 1, :], shape)

    groups = BLOCK // 8
    rows = [block[8 * g : 8 * g + 8, :] for g in range(groups)]
    done = []
    for b in range(groups):
        k = 8 * b
        own = rows[b]
        inside = (lane >= k) & (lane < k + 8)
        columns = [along_lanes(own, k + j) for j in range(8)]
        entry = {(i, j): along_rows(columns[j], i) for j in range(8) for i in range(j, 8)}
        unit = jnp.where(inside, (lane - k == sub).astype(jnp.float32), own)
        line = [along_rows(unit, i) for i in range(8)]
        last = b == groups - 1
        if not last:
            following = rows[b + 1]
            mults = [along_lanes(following, k + j) for j in range(8)]
            following = jnp.where(inside, 0.0, following)
        scale, low = [], {}
        for j in range(8):
            r = lax.rsqrt(entry[j, j])
            scale.append(r)
            for i in range(j + 1, 8):
                low[i, j] = entry[i, j] * r
            for i in range(j + 1, 8):
                for m in range(j + 1, i + 1):
                    entry[i, m] = entry[i, m] - low[i, j] * low[m, j]
            line[j] = line[j] * r
            for i in range(j + 1, 8):
                line[i] = line[i] - low[i, j] * line[j]
            if not last:
                mults[j] = mults[j] * r
                for i in range(j + 1, 8):
                    mults[i] = mults[i] - low[i, j] * mults[j]
                following = following - mults[j] * line[j]
        compact = line[0]
        for j in range(1, 8):
            compact = jnp.where(sub == j, line[j], compact)
        done.append(jnp.where(lane <= k + sub, compact, 0.0))
        if not last:
            rows[b + 1] = following
        if b + 2 < groups:
            back = [None] * 8
            for j in range(7, -1, -1):
                total = line[j]
                for i in range(j + 1, 8):
                    total = total - low[i, j] * back[i]
                back[j] = total * scale[j]
            for g in range(b + 2, groups):
                target = rows[g]
                left = [along_lanes(target, k + j) for j in range(8)]
                target = jnp.where(inside, 0.0, target)
                for j in range(8):
                    target = target - left[j] * back[j]
                rows[g] = target
        for task in tasks[b]:
            task()
    return jnp.concatenate(done, axis=0)


def spans(start, stop, size):
    return [(at, min(size, stop - at)) for at in range(start, stop, size)]


def panel_kernel(index, count, share, effects, skipped, *refs):
    nodes = 2 * share
    last = index == count - 1
    inputs, refs = refs[: 6 + 2 * index], refs[6 + 2 * index :]
    where_ref, open_ref, diag_ref, coup_ref, arrow_ref, other_ref = inputs[:6]
    earlier = inputs[6:]
    refs = refs[skipped:]
    factor_ref, first_ref, second_ref, third_ref, send_ref, cross_ref, high_ref, low_ref = refs[:8]
    if last:
        corner_ref = refs[8]
    work, stage, turned, factor, high, low, high_before, low_before, sems, before_sems, out_sems = refs[8 + last :]
    member = where_ref[0]
    start = index * PANEL
    square = nodes - start
    total = square + 2 * share + 2 * effects
    columns = pl.ds(start, PANEL)
    second_at, first_at, third_at = square, square + share, square + 2 * share

    holder, inner = divmod(start, share)
    held = share - inner
    rest = square - held

    def split_copies(owner):
        if owner == holder:
            pairs = [
                (diag_ref.at[1, pl.ds(inner, held), columns], work.at[pl.ds(0, held)]),
                (coup_ref.at[0, pl.ds(inner, PANEL), pl.ds(owner * share, share)], stage),
            ]
            if rest:
                pairs.append((diag_ref.at[1, pl.ds(inner, PANEL), pl.ds(share, share)], turned))
        else:
            pairs = [(other_ref.at[pl.ds(inner, held)], work.at[pl.ds(0, held)])]
            for c in range(0, share, PANEL):
                pairs.append((other_ref.at[pl.ds(share + c, PANEL)], stage.at[:, pl.ds(c, PANEL)]))
            if rest:
                pairs.append((diag_ref.at[1, :, columns], work.at[pl.ds(held, rest)]))
        return [pltpu.make_async_copy(*pair, sems.at[n]) for n, pair in enumerate(pairs)]

    for owner in range(2):
        @pl.when(member == owner)
        def _():
            for copy in split_copies(owner):
                copy.start()

    same = [
        pltpu.make_async_copy(coup_ref.at[1, :, columns], work.at[pl.ds(second_at, share)], sems.at[4]),
        pltpu.make_async_copy(arrow_ref.at[1, :, columns], work.at[pl.ds(third_at, effects)], sems.at[5]),
        pltpu.make_async_copy(
            other_ref.at[pl.ds(nodes + holder * effects, effects)], work.at[pl.ds(third_at + effects, effects)], sems.at[6]
        ),
    ]
    for j in range(index):
        skip = start - j * PANEL
        for n, (source, target) in enumerate(((earlier[2 * j], high_before), (earlier[2 * j + 1], low_before))):
            same.append(
                pltpu.make_async_copy(source.at[pl.ds(skip, total)], target.at[j], before_sems.at[2 * j + n])
            )
    for copy in same:
        copy.start()
    if start:
        factor[0:start, :] = jnp.zeros((start, PANEL), jnp.float32)
    for owner in range(2):
        @pl.when(member == owner)
        def _():
            for copy in split_copies(owner):
                copy.wait()
            if owner == holder and rest:
                for r in range(0, PANEL, BLOCK):
                    for c in range(0, rest, BLOCK):
                        work[held + c : held + c + BLOCK, r : r + BLOCK] = turned[r : r + BLOCK, c : c + BLOCK].T

    for copy in same:
        copy.wait()

    @pl.when(open_ref[0] == 0)
    def _():
        work[second_at : second_at + share, :] = jnp.zeros((share, PANEL), jnp.float32)

    for r in range(0, PANEL, BLOCK):
        for c in range(0, share, BLOCK):
            work[first_at + c : first_at + c + BLOCK, r : r + BLOCK] = stage[r : r + BLOCK, c : c + BLOCK].T

    def update(at, size):
        if not index:
            return
        value = work[at : at + size, :]
        for j in range(index):
            left = left_terms(high_before[j, at : at + size, :], low_before[j, at : at + size, :])
            right = right_terms(high_before[j, 0:PANEL, :], low_before[j, 0:PANEL, :])
            value = value - plain_nt(left, right)
        work[at : at + size, :] = value

    update(0, PANEL)
    waiting = spans(PANEL, total, BLOCK)
    tasks = [[] for _ in range(32)]
    for n, (at, size) in enumerate(waiting):
        tasks[(32 * n) // len(waiting)].append(functools.partial(update, at, size))

    head = work[0:BLOCK, 0:BLOCK]
    side = work[BLOCK:PANEL, 0:BLOCK]
    tail = work[BLOCK:PANEL, BLOCK:PANEL]
    head_inverse = inverse_of_factor(head, tasks[:16])
    beside = exact(side, head_inverse, 1)
    across = exact(beside, head_inverse, 0)
    tail_inverse = inverse_of_factor(tail - exact(beside, beside, 1), tasks[16:])
    corner = -exact(tail_inverse, across, 0)
    inverse = jnp.concatenate(
        [
            jnp.concatenate([head_inverse, jnp.zeros((BLOCK, BLOCK), jnp.float32)], axis=1),
            jnp.concatenate([corner, tail_inverse], axis=1),
        ],
        axis=0,
    )
    right = right_terms(*split(inverse))

    def solve(at, size):
        solved = plain_nt(left_terms(*split(work[at : at + size, :])), right)
        if at < PANEL:
            row = lax.broadcasted_iota(jnp.int32, solved.shape, 0) + at
            lane = lax.broadcasted_iota(jnp.int32, solved.shape, 1)
            solved = jnp.where(row >= lane, solved, 0.0)
        if at < square:
            factor[start + at : start + at + size, :] = solved
        else:
            work[at : at + size, :] = solved
        high[at : at + size, :], low[at : at + size, :] = split(solved)

    sends = [
        (work.at[pl.ds(second_at, 2 * share + effects)], send_ref),
        (work.at[pl.ds(first_at, share)], cross_ref),
        (work.at[pl.ds(first_at, share)], first_ref.at[0, :, columns]),
        (work.at[pl.ds(second_at, share)], second_ref.at[0, :, columns]),
        (work.at[pl.ds(third_at, effects)], third_ref.at[0, :, columns]),
        (factor.at[pl.ds(pl.multiple_of(member * share, share), share)], factor_ref.at[0, :, columns]),
        (high, high_ref),
        (low, low_ref),
    ]
    sends = [pltpu.make_async_copy(source, target, out_sems.at[n]) for n, (source, target) in enumerate(sends)]
    for at, size in spans(square, total, PANEL):
        solve(at, size)
    for copy in sends[:5]:
        copy.start()
    for at, size in spans(0, square, PANEL):
        solve(at, size)
    for copy in sends[5:]:
        copy.start()
    if last:
        at, size = third_at, 2 * effects
        value = plain_nt(
            left_terms(high[at : at + effects, :], low[at : at + effects, :]),
            right_terms(high[at : at + size, :], low[at : at + size, :]),
        )
        for j in range(index):
            value = value + plain_nt(
                left_terms(high_before[j, at : at + effects, :], low_before[j, at : at + effects, :]),
                right_terms(high_before[j, at : at + size, :], low_before[j, at : at + size, :]),
            )
        crossed = jnp.concatenate([value[:, effects:], value[:, :effects]], axis=1)
        corner_ref[...] = jnp.where(member == 0, value, crossed)
    for copy in sends:
        copy.wait()


def panel(index, inputs, earlier, results, order):
    member, opened, diag_block, coupling, arrow, other = inputs
    share, nodes = diag_block.shape[1:]
    effects = arrow.shape[1]
    count = nodes // PANEL
    total = nodes - index * PANEL + 2 * share + 2 * effects
    anywhere = pl.BlockSpec(memory_space=pl.ANY)
    scalar = pl.BlockSpec(memory_space=pltpu.SMEM)
    shapes = [
        ((1, share, nodes), jnp.float32), ((1, share, nodes), jnp.float32),
        ((1, share, nodes), jnp.float32), ((1, effects, nodes), jnp.float32),
        ((2 * share + effects, PANEL), jnp.float32), ((share, PANEL), jnp.float32),
        ((total, PANEL), jnp.bfloat16), ((total, PANEL), jnp.bfloat16),
    ]
    outs = [anywhere] * len(shapes)
    if index == count - 1:
        shapes.append(((effects, 2 * effects), jnp.float32))
        outs.append(pl.BlockSpec(memory_space=pltpu.VMEM))
    operands = [*inputs, *earlier, *results, *order]
    aliases = {6 + len(earlier) + n: n for n in range(len(results))}
    return pl.pallas_call(
        functools.partial(panel_kernel, index, count, share, effects, len(results) + len(order)),
        out_shape=[jax.ShapeDtypeStruct(shape, kind) for shape, kind in shapes],
        in_specs=[scalar, scalar] + [anywhere] * (len(operands) - 2),
        out_specs=outs,
        scratch_shapes=[
            pltpu.VMEM((total, PANEL), jnp.float32),
            pltpu.VMEM((PANEL, share), jnp.float32),
            pltpu.VMEM((PANEL, share), jnp.float32),
            pltpu.VMEM((nodes, PANEL), jnp.float32),
            pltpu.VMEM((total, PANEL), jnp.bfloat16),
            pltpu.VMEM((total, PANEL), jnp.bfloat16),
            pltpu.VMEM((max(index, 1), total, PANEL), jnp.bfloat16),
            pltpu.VMEM((max(index, 1), total, PANEL), jnp.bfloat16),
            pltpu.SemaphoreType.DMA((7,)),
            pltpu.SemaphoreType.DMA((max(2 * index, 1),)),
            pltpu.SemaphoreType.DMA((8,)),
        ],
        input_output_aliases=aliases,
        compiler_params=pltpu.CompilerParams(vmem_limit_bytes=56 * 1024 * 1024),
        cost_estimate=SMALL,
        name=f"panel_{index}",
    )(*operands)


def exchange_kernel(where_ref, diag_ref, coup_ref, arrow_ref, *refs):
    outs, sems = refs[:-1], refs[-1]
    share, nodes = diag_ref.shape[1:]
    effects = arrow_ref.shape[1]
    member = where_ref[0]
    own_at = pl.multiple_of(member * share, share)
    other_at = pl.multiple_of((1 - member) * share, share)
    copies = []
    for n, out in enumerate(outs):
        pairs = [(diag_ref.at[1, :, pl.ds(own_at + n * PANEL, PANEL)], out.at[pl.ds(0, share)])]
        for c in range(0, share, PANEL):
            pairs.append(
                (coup_ref.at[0, pl.ds(n * PANEL, PANEL), pl.ds(other_at + c, PANEL)], out.at[pl.ds(share + c, PANEL)])
            )
        for m in range(2):
            source = arrow_ref.at[1, :, pl.ds(m * share + n * PANEL, PANEL)]
            pairs.append((source, out.at[pl.ds(nodes + m * effects, effects)]))
        for source, target in pairs:
            copies.append(pltpu.make_async_copy(source, target, sems.at[len(copies)]))
    for copy in copies:
        copy.start()
    for copy in copies:
        copy.wait()


def exchange(member, diag_block, coupling, arrow):
    share, nodes = diag_block.shape[1:]
    effects = arrow.shape[1]
    count = share // PANEL
    rows = nodes + 2 * effects
    anywhere = pl.BlockSpec(memory_space=pl.ANY)
    return pl.pallas_call(
        exchange_kernel,
        out_shape=[jax.ShapeDtypeStruct((rows, PANEL), jnp.float32)] * count,
        in_specs=[pl.BlockSpec(memory_space=pltpu.SMEM)] + [anywhere] * 3,
        out_specs=[pl.BlockSpec(memory_space=pltpu.VMEM)] * count,
        scratch_shapes=[pltpu.SemaphoreType.DMA((count * (3 + count),))],
        compiler_params=pltpu.CompilerParams(vmem_limit_bytes=56 * 1024 * 1024),
        cost_estimate=SMALL,
        name="exchange",
    )(member, diag_block, coupling, arrow)


def own_products_kernel(half, count, share, effects, skipped, *refs):
    where_ref, diag_ref, arrow_ref = refs[:3]
    highs, lows, refs = refs[3 : 3 + count], refs[3 + count : 3 + 2 * count], refs[3 + 2 * count :]
    if half:
        crosses, refs = refs[:count], refs[count:]
    refs = refs[skipped:]
    pivot_ref, right_ref, arrow_out_ref = refs[:3]
    high, low, other, pivot, middle, lines, sems, out_sems = refs[3:]
    member = where_ref[0]
    rows = 2 * share + effects
    columns = pl.ds(pl.multiple_of((1 - member if half else member) * share, share), share)
    copies = []
    for n in range(count):
        skip = highs[n].shape[0] - rows - effects
        copies.append(pltpu.make_async_copy(highs[n].at[pl.ds(skip, rows)], high.at[n], sems.at[3 * n]))
        copies.append(pltpu.make_async_copy(lows[n].at[pl.ds(skip, rows)], low.at[n], sems.at[3 * n + 1]))
        if half:
            copies.append(pltpu.make_async_copy(crosses[n], other.at[n], sems.at[3 * n + 2]))
    copies.append(pltpu.make_async_copy(diag_ref.at[0, :, columns], pivot, sems.at[3 * count]))
    copies.append(pltpu.make_async_copy(arrow_ref.at[0, :, columns], lines, sems.at[3 * count + 1]))
    for copy in copies:
        copy.start()
    for copy in copies:
        copy.wait()
    for c in range(0, share, PANEL):
        if half:
            right = [right_terms(*split(other[n, c : c + PANEL, :])) for n in range(count)]
        else:
            right = [
                right_terms(high[n, share + c : share + c + PANEL, :], low[n, share + c : share + c + PANEL, :])
                for n in range(count)
            ]
        for at, size in spans(0, rows, PANEL):
            value = 0.0
            for n in range(count):
                left = left_terms(high[n, at : at + size, :], low[n, at : at + size, :])
                value = value + plain_nt(left, right[n])
            if at < share:
                middle[at : at + size, c : c + PANEL] = -value
            elif at < 2 * share:
                to = at - share
                pivot[to : to + size, c : c + PANEL] = pivot[to : to + size, c : c + PANEL] - value
            else:
                lines[:, c : c + PANEL] = lines[:, c : c + PANEL] - value
    results = [
        (pivot, pivot_ref.at[:, columns]), (middle, right_ref.at[0, :, columns]), (lines, arrow_out_ref.at[:, columns])
    ]
    results = [pltpu.make_async_copy(source, target, out_sems.at[n]) for n, (source, target) in enumerate(results)]
    for copy in results:
        copy.start()
    for copy in results:
        copy.wait()


def own_products(half, member, diag_block, arrow, highs, lows, crosses, before):
    share, nodes = diag_block.shape[1:]
    effects = arrow.shape[1]
    count = len(highs)
    rows = 2 * share + effects
    anywhere = pl.BlockSpec(memory_space=pl.ANY)
    scalar = pl.BlockSpec(memory_space=pltpu.SMEM)
    shapes = [(share, nodes), (1, share, nodes), (effects, nodes)]
    operands = [member, diag_block, arrow, *highs, *lows, *crosses]
    aliases = {len(operands) + n: n for n in range(len(before))}
    operands += before
    return pl.pallas_call(
        functools.partial(own_products_kernel, half, count, share, effects, len(before)),
        out_shape=[jax.ShapeDtypeStruct(shape, jnp.float32) for shape in shapes],
        in_specs=[scalar] + [anywhere] * (len(operands) - 1),
        out_specs=[anywhere] * 3,
        scratch_shapes=[
            pltpu.VMEM((count, rows, PANEL), jnp.bfloat16),
            pltpu.VMEM((count, rows, PANEL), jnp.bfloat16),
            pltpu.VMEM((count, share, PANEL), jnp.float32),
            pltpu.VMEM((share, share), jnp.float32),
            pltpu.VMEM((share, share), jnp.float32),
            pltpu.VMEM((effects, share), jnp.float32),
            pltpu.SemaphoreType.DMA((3 * count + 2,)),
            pltpu.SemaphoreType.DMA((3,)),
        ],
        input_output_aliases=aliases,
        compiler_params=pltpu.CompilerParams(vmem_limit_bytes=56 * 1024 * 1024),
        cost_estimate=SMALL,
        name=f"own_products_{half}",
    )(*operands)


def next_products_kernel(count, with_left, share, effects, *refs):
    where_ref, pivot_in, arrow_in = refs[:3]
    refs = refs[3:]
    if with_left:
        left_in, refs = refs[0], refs[1:]
    owns, others = refs[:count], refs[count : 2 * count]
    refs = refs[2 * count :]
    pivot_ref, left_ref, arrow_ref = refs[:3]
    own, other, pivot, middle, lines, sems, out_sems = refs[3:]
    member = where_ref[0]
    rows = 2 * share + effects
    copies = []
    for n in range(count):
        copies.append(pltpu.make_async_copy(owns[n], own.at[n], sems.at[2 * n]))
        copies.append(pltpu.make_async_copy(others[n], other.at[n], sems.at[2 * n + 1]))
    copies.append(pltpu.make_async_copy(pivot_in, pivot, sems.at[2 * count]))
    copies.append(pltpu.make_async_copy(arrow_in, lines, sems.at[2 * count + 1]))
    if with_left:
        copies.append(pltpu.make_async_copy(left_in, middle, sems.at[2 * count + 2]))
    for copy in copies:
        copy.start()
    for copy in copies:
        copy.wait()
    own_at = pl.multiple_of(member * share, share)
    other_at = pl.multiple_of((1 - member) * share, share)
    right = [
        [
            [right_terms(*split(source[n, c : c + PANEL, :])) for n in range(count)]
            for c in range(0, share, PANEL)
        ]
        for source in (own, other)
    ]
    for at, size in spans(0, rows, PANEL):
        left = [left_terms(*split(own[n, at : at + size, :])) for n in range(count)]
        for half, base in ((0, own_at), (1, other_at)):
            for c in range(0, share, PANEL):
                columns = pl.ds(pl.multiple_of(base + c, PANEL), PANEL)
                value = 0.0
                for n in range(count):
                    value = value + plain_nt(left[n], right[half][c // PANEL][n])
                if at < share:
                    pivot[at : at + size, columns] = pivot[at : at + size, columns] - value
                elif at < 2 * share:
                    to = at - share
                    if with_left:
                        middle[to : to + size, columns] = middle[to : to + size, columns] - value
                    else:
                        middle[to : to + size, columns] = -value
                else:
                    lines[:, columns] = lines[:, columns] - value
    results = [(pivot, pivot_ref), (middle, left_ref), (lines, arrow_ref)]
    results = [pltpu.make_async_copy(source, target, out_sems.at[n]) for n, (source, target) in enumerate(results)]
    for copy in results:
        copy.start()
    for copy in results:
        copy.wait()


def next_products(member, pivot, arrow, left, owns, others):
    share, nodes = pivot.shape
    effects = arrow.shape[0]
    count = len(owns)
    rows = 2 * share + effects
    anywhere = pl.BlockSpec(memory_space=pl.ANY)
    scalar = pl.BlockSpec(memory_space=pltpu.SMEM)
    with_left = left is not None
    operands = [member, pivot, arrow] + ([left] if with_left else []) + [*owns, *others]
    shapes = [(share, nodes), (share, nodes), (effects, nodes)]
    return pl.pallas_call(
        functools.partial(next_products_kernel, count, with_left, share, effects),
        out_shape=[jax.ShapeDtypeStruct(shape, jnp.float32) for shape in shapes],
        in_specs=[scalar] + [anywhere] * (len(operands) - 1),
        out_specs=[anywhere] * 3,
        scratch_shapes=[
            pltpu.VMEM((count, rows, PANEL), jnp.float32),
            pltpu.VMEM((count, share, PANEL), jnp.float32),
            pltpu.VMEM((share, nodes), jnp.float32),
            pltpu.VMEM((share, nodes), jnp.float32),
            pltpu.VMEM((effects, nodes), jnp.float32),
            pltpu.SemaphoreType.DMA((2 * count + 3,)),
            pltpu.SemaphoreType.DMA((3,)),
        ],
        compiler_params=pltpu.CompilerParams(vmem_limit_bytes=24 * 1024 * 1024),
        cost_estimate=SMALL,
        name=f"next_products_{count}",
    )(*operands)


def local(diag_block, coupling, arrow, corner):
    partition_count = lax.axis_size("tm")
    position = lax.axis_index("tm")
    at = lax.axis_index("blk").astype(jnp.int32)
    member = at.reshape((1,))
    opened = (position < partition_count - 1).astype(jnp.int32).reshape((1,))
    share, nodes = diag_block.shape[1:]
    halves = [swapped(part) for part in exchange(member, diag_block, coupling, arrow)]
    earlier, results, highs, lows, crosses, owns, others = [], [], [], [], [], [], []
    for index in range(nodes // PANEL):
        inputs = (member, opened, diag_block, coupling, arrow, halves[index % len(halves)])
        order = []
        if index > 1:
            order = [owns[index - 2], crosses[index - 2], *others[index - 3 : index - 2]]
        found = panel(index, inputs, earlier, results, order)
        results = found[:4]
        send, cross, high, low = found[4:8]
        earlier += [high, low]
        highs.append(high)
        lows.append(low)
        owns.append(shifted(send, "tm", 1))
        crosses.append(swapped(cross))
        if index < nodes // PANEL - 2:
            others.append(swapped(owns[-1][:share]))
    total = found[8]
    even = partition_count & (partition_count - 1) == 0
    steps = partition_count // 2
    if not even:
        total = lax.psum(total, "tm")
    products = own_products(0, member, diag_block, arrow, highs, lows, [], [])
    owns[-2] = after(owns[-2], products[0])
    others.append(swapped(owns[-2][:share]))
    if even and steps:
        total = paired_sum(total, "tm", steps, products[0])
    products = own_products(1, member, diag_block, arrow, highs, lows, crosses, products)
    steps //= 2
    if even and steps:
        total = paired_sum(total, "tm", steps, products[0])
    pivot, right_out, lines = products
    pivot, left, lines = next_products(member, pivot, lines, None, owns[:-1], others)
    steps //= 2
    while even and steps:
        total = paired_sum(total, "tm", steps, pivot)
        steps //= 2
    final = after(owns[-1], pivot, total)
    pivot, left, lines = next_products(member, pivot, lines, left, [final], [swapped(final[:share])])
    corner_out = corner - total
    return (*results, pivot[None], left[None], right_out, lines[None], corner_out)


def solution(mesh):
    placed = (P("tm", "blk", None), P("tm", "blk", None), P("tm", "blk", None), P("blk", None))
    return jax.shard_map(
        local,
        mesh=mesh,
        in_specs=placed,
        out_specs=(P("tm", "blk", None),) * 8 + (P("blk", None),),
        check_vma=False,
    )
```

```python
import functools

import jax
import jax.numpy as jnp
from jax import lax
from jax.experimental import pallas as pl
from jax.experimental.pallas import tpu as pltpu
from jax.sharding import PartitionSpec as P

BLOCK = 128
PANEL = 256
SMALL = pl.CostEstimate(flops=10**6, bytes_accessed=10**4, transcendentals=0)


def shifted(value, axis, steps):
    count = lax.axis_size(axis)
    leading, last = (max(0, -steps), min(count, count - steps))
    return lax.ppermute(value, axis, [(source, source + steps) for source in range(leading, last)])


def swapped(value):
    return lax.ppermute(value, "blk", [(0, 1), (1, 0)])


def after(value, *earlier):
    return lax.optimization_barrier((value, *earlier))[0]


def corner_rounds(count):
    rounds, steps = [], 1
    while count % 2 == 0:
        size = 4 if count % 4 == 0 else 2
        rounds.append((steps, size))
        steps, count = steps * size, count // size
    return rounds if count == 1 else []


def grouped_sum(value, axis, steps, size, *earlier):
    count = lax.axis_size(axis)
    found = [
        lax.ppermute(value, axis, [(source, source ^ (other * steps)) for source in range(count)])
        for other in range(1, size)
    ]
    found = lax.optimization_barrier((*found, *earlier))[: size - 1]
    value = value + found[0]
    return value + (found[1] + found[2]) if size == 4 else value


def exact(left, right, right_dim):
    return lax.dot_general(
        left, right, (((1,), (right_dim,)), ((), ())), precision=lax.Precision.HIGHEST, preferred_element_type=jnp.float32
    )


def plain_nt(left, right):
    return lax.dot_general(left, right, (((1,), (1,)), ((), ())), preferred_element_type=jnp.float32)


def split(value):
    high = value.astype(jnp.bfloat16)
    low = (value - high.astype(jnp.float32)).astype(jnp.bfloat16)
    return high, low


def left_terms(high, low):
    return jnp.concatenate([high, low, high], axis=1)


def right_terms(high, low):
    return jnp.concatenate([high, high, low], axis=1)


def inverse_of_factor(block, tasks):
    shape = (8, BLOCK)
    lane = lax.broadcasted_iota(jnp.int32, shape, 1)
    sub = lax.broadcasted_iota(jnp.int32, shape, 0)

    def along_lanes(value, at):
        return jnp.broadcast_to(value[:, at : at + 1], shape)

    def along_rows(value, at):
        return jnp.broadcast_to(value[at : at + 1, :], shape)

    groups = BLOCK // 8
    rows = [block[8 * g : 8 * g + 8, :] for g in range(groups)]
    done = []
    for b in range(groups):
        k = 8 * b
        own = rows[b]
        inside = (lane >= k) & (lane < k + 8)
        columns = [along_lanes(own, k + j) for j in range(8)]
        entry = {(i, j): along_rows(columns[j], i) for j in range(8) for i in range(j, 8)}
        unit = jnp.where(inside, (lane - k == sub).astype(jnp.float32), own)
        line = [along_rows(unit, i) for i in range(8)]
        last = b == groups - 1
        if not last:
            following = rows[b + 1]
            mults = [along_lanes(following, k + j) for j in range(8)]
            following = jnp.where(inside, 0.0, following)
        scale, low = [], {}
        for j in range(8):
            r = lax.rsqrt(entry[j, j])
            scale.append(r)
            for i in range(j + 1, 8):
                low[i, j] = entry[i, j] * r
            for i in range(j + 1, 8):
                for m in range(j + 1, i + 1):
                    entry[i, m] = entry[i, m] - low[i, j] * low[m, j]
            line[j] = line[j] * r
            for i in range(j + 1, 8):
                line[i] = line[i] - low[i, j] * line[j]
            if not last:
                mults[j] = mults[j] * r
                for i in range(j + 1, 8):
                    mults[i] = mults[i] - low[i, j] * mults[j]
                following = following - mults[j] * line[j]
        compact = line[0]
        for j in range(1, 8):
            compact = jnp.where(sub == j, line[j], compact)
        done.append(jnp.where(lane <= k + sub, compact, 0.0))
        if not last:
            rows[b + 1] = following
        if b + 2 < groups:
            back = [None] * 8
            for j in range(7, -1, -1):
                total = line[j]
                for i in range(j + 1, 8):
                    total = total - low[i, j] * back[i]
                back[j] = total * scale[j]
            for g in range(b + 2, groups):
                target = rows[g]
                left = [along_lanes(target, k + j) for j in range(8)]
                target = jnp.where(inside, 0.0, target)
                for j in range(8):
                    target = target - left[j] * back[j]
                rows[g] = target
        for task in tasks[b]:
            task()
    return jnp.concatenate(done, axis=0)


def spans(start, stop, size):
    return [(at, min(size, stop - at)) for at in range(start, stop, size)]


def panel_kernel(index, count, share, effects, skipped, *refs):
    nodes = 2 * share
    last = index == count - 1
    inputs, refs = refs[: 6 + 2 * index], refs[6 + 2 * index :]
    where_ref, open_ref, diag_ref, coup_ref, arrow_ref, other_ref = inputs[:6]
    earlier = inputs[6:]
    refs = refs[skipped:]
    factor_ref, first_ref, second_ref, third_ref, send_ref, cross_ref, high_ref, low_ref = refs[:8]
    if last:
        corner_ref = refs[8]
    work, stage, turned, factor, high, low, high_before, low_before, sems, before_sems, out_sems = refs[8 + last :]
    member = where_ref[0]
    start = index * PANEL
    square = nodes - start
    total = square + 2 * share + 2 * effects
    columns = pl.ds(start, PANEL)
    second_at, first_at, third_at = square, square + share, square + 2 * share

    holder, inner = divmod(start, share)
    held = share - inner
    rest = square - held

    def split_copies(owner):
        if owner == holder:
            pairs = [
                (diag_ref.at[1, pl.ds(inner, held), columns], work.at[pl.ds(0, held)]),
                (coup_ref.at[0, pl.ds(inner, PANEL), pl.ds(owner * share, share)], stage),
            ]
            if rest:
                pairs.append((diag_ref.at[1, pl.ds(inner, PANEL), pl.ds(share, share)], turned))
        else:
            pairs = [(other_ref.at[pl.ds(inner, held)], work.at[pl.ds(0, held)])]
            for c in range(0, share, PANEL):
                pairs.append((other_ref.at[pl.ds(share + c, PANEL)], stage.at[:, pl.ds(c, PANEL)]))
            if rest:
                pairs.append((diag_ref.at[1, :, columns], work.at[pl.ds(held, rest)]))
        return [pltpu.make_async_copy(*pair, sems.at[n]) for n, pair in enumerate(pairs)]

    for owner in range(2):
        @pl.when(member == owner)
        def _():
            for copy in split_copies(owner):
                copy.start()

    same = [
        pltpu.make_async_copy(coup_ref.at[1, :, columns], work.at[pl.ds(second_at, share)], sems.at[4]),
        pltpu.make_async_copy(arrow_ref.at[1, :, columns], work.at[pl.ds(third_at, effects)], sems.at[5]),
        pltpu.make_async_copy(
            other_ref.at[pl.ds(nodes + holder * effects, effects)], work.at[pl.ds(third_at + effects, effects)], sems.at[6]
        ),
    ]
    first = []
    for j in range(index):
        skip = start - j * PANEL
        for n, (source, target) in enumerate(((earlier[2 * j], high_before), (earlier[2 * j + 1], low_before))):
            for copies, at, size in ((first, 0, PANEL), (same, PANEL, total - PANEL)):
                sem = before_sems.at[4 * j + 2 * n + (at > 0)]
                copies.append(
                    pltpu.make_async_copy(source.at[pl.ds(skip + at, size)], target.at[j, pl.ds(at, size)], sem)
                )
    for copy in first + same:
        copy.start()
    if start:
        factor[0:start, :] = jnp.zeros((start, PANEL), jnp.float32)
    def update(at, size):
        if not index:
            return
        value = work[at : at + size, :]
        for j in range(index):
            left = left_terms(high_before[j, at : at + size, :], low_before[j, at : at + size, :])
            right = right_terms(high_before[j, 0:PANEL, :], low_before[j, 0:PANEL, :])
            value = value - plain_nt(left, right)
        work[at : at + size, :] = value

    split_copies(0)[0].wait()
    for copy in first:
        copy.wait()
    update(0, PANEL)
    for owner in range(2):
        @pl.when(member == owner)
        def _():
            for copy in split_copies(owner)[1:]:
                copy.wait()
            if owner == holder and rest:
                for r in range(0, PANEL, BLOCK):
                    for c in range(0, rest, BLOCK):
                        work[held + c : held + c + BLOCK, r : r + BLOCK] = turned[r : r + BLOCK, c : c + BLOCK].T

    for copy in same:
        copy.wait()

    @pl.when(open_ref[0] == 0)
    def _():
        work[second_at : second_at + share, :] = jnp.zeros((share, PANEL), jnp.float32)

    for r in range(0, PANEL, BLOCK):
        for c in range(0, share, BLOCK):
            work[first_at + c : first_at + c + BLOCK, r : r + BLOCK] = stage[r : r + BLOCK, c : c + BLOCK].T

    waiting = spans(PANEL, total, BLOCK)
    tasks = [[] for _ in range(32)]
    for n, (at, size) in enumerate(waiting):
        tasks[(32 * n) // len(waiting)].append(functools.partial(update, at, size))

    head = work[0:BLOCK, 0:BLOCK]
    side = work[BLOCK:PANEL, 0:BLOCK]
    tail = work[BLOCK:PANEL, BLOCK:PANEL]
    head_inverse = inverse_of_factor(head, tasks[:16])
    beside = exact(side, head_inverse, 1)
    across = exact(beside, head_inverse, 0)
    tail_inverse = inverse_of_factor(tail - exact(beside, beside, 1), tasks[16:])
    corner = -exact(tail_inverse, across, 0)
    inverse = jnp.concatenate(
        [
            jnp.concatenate([head_inverse, jnp.zeros((BLOCK, BLOCK), jnp.float32)], axis=1),
            jnp.concatenate([corner, tail_inverse], axis=1),
        ],
        axis=0,
    )
    right = right_terms(*split(inverse))

    def solve(at, size):
        solved = plain_nt(left_terms(*split(work[at : at + size, :])), right)
        if at < PANEL:
            row = lax.broadcasted_iota(jnp.int32, solved.shape, 0) + at
            lane = lax.broadcasted_iota(jnp.int32, solved.shape, 1)
            solved = jnp.where(row >= lane, solved, 0.0)
        if at < square:
            factor[start + at : start + at + size, :] = solved
        else:
            work[at : at + size, :] = solved
        high[at : at + size, :], low[at : at + size, :] = split(solved)

    sends = [
        (work.at[pl.ds(second_at, 2 * share + effects)], send_ref),
        (work.at[pl.ds(first_at, share)], cross_ref),
        (work.at[pl.ds(first_at, share)], first_ref.at[0, :, columns]),
        (work.at[pl.ds(second_at, share)], second_ref.at[0, :, columns]),
        (work.at[pl.ds(third_at, effects)], third_ref.at[0, :, columns]),
        (factor.at[pl.ds(pl.multiple_of(member * share, share), share)], factor_ref.at[0, :, columns]),
        (high, high_ref),
        (low, low_ref),
    ]
    sends = [pltpu.make_async_copy(source, target, out_sems.at[n]) for n, (source, target) in enumerate(sends)]
    for at, size in spans(square, total, PANEL):
        solve(at, size)
    for copy in sends[:5]:
        copy.start()
    for at, size in spans(0, square, PANEL):
        solve(at, size)
    for copy in sends[5:]:
        copy.start()
    if last:
        at, size = third_at, 2 * effects
        value = plain_nt(
            left_terms(high[at : at + effects, :], low[at : at + effects, :]),
            right_terms(high[at : at + size, :], low[at : at + size, :]),
        )
        for j in range(index):
            value = value + plain_nt(
                left_terms(high_before[j, at : at + effects, :], low_before[j, at : at + effects, :]),
                right_terms(high_before[j, at : at + size, :], low_before[j, at : at + size, :]),
            )
        crossed = jnp.concatenate([value[:, effects:], value[:, :effects]], axis=1)
        corner_ref[...] = jnp.where(member == 0, value, crossed)
    for copy in sends:
        copy.wait()


def panel(index, inputs, earlier, results, order):
    member, opened, diag_block, coupling, arrow, other = inputs
    share, nodes = diag_block.shape[1:]
    effects = arrow.shape[1]
    count = nodes // PANEL
    total = nodes - index * PANEL + 2 * share + 2 * effects
    anywhere = pl.BlockSpec(memory_space=pl.ANY)
    scalar = pl.BlockSpec(memory_space=pltpu.SMEM)
    shapes = [
        ((1, share, nodes), jnp.float32), ((1, share, nodes), jnp.float32),
        ((1, share, nodes), jnp.float32), ((1, effects, nodes), jnp.float32),
        ((2 * share + effects, PANEL), jnp.float32), ((share, PANEL), jnp.float32),
        ((total, PANEL), jnp.bfloat16), ((total, PANEL), jnp.bfloat16),
    ]
    outs = [anywhere] * len(shapes)
    if index == count - 1:
        shapes.append(((effects, 2 * effects), jnp.float32))
        outs.append(pl.BlockSpec(memory_space=pltpu.VMEM))
    operands = [*inputs, *earlier, *results, *order]
    aliases = {6 + len(earlier) + n: n for n in range(len(results))}
    return pl.pallas_call(
        functools.partial(panel_kernel, index, count, share, effects, len(results) + len(order)),
        out_shape=[jax.ShapeDtypeStruct(shape, kind) for shape, kind in shapes],
        in_specs=[scalar, scalar] + [anywhere] * (len(operands) - 2),
        out_specs=outs,
        scratch_shapes=[
            pltpu.VMEM((total, PANEL), jnp.float32),
            pltpu.VMEM((PANEL, share), jnp.float32),
            pltpu.VMEM((PANEL, share), jnp.float32),
            pltpu.VMEM((nodes, PANEL), jnp.float32),
            pltpu.VMEM((total, PANEL), jnp.bfloat16),
            pltpu.VMEM((total, PANEL), jnp.bfloat16),
            pltpu.VMEM((max(index, 1), total, PANEL), jnp.bfloat16),
            pltpu.VMEM((max(index, 1), total, PANEL), jnp.bfloat16),
            pltpu.SemaphoreType.DMA((7,)),
            pltpu.SemaphoreType.DMA((max(4 * index, 1),)),
            pltpu.SemaphoreType.DMA((8,)),
        ],
        input_output_aliases=aliases,
        compiler_params=pltpu.CompilerParams(vmem_limit_bytes=40 * 1024 * 1024),
        cost_estimate=SMALL,
        name=f"panel_{index}",
    )(*operands)


def exchange_kernel(where_ref, diag_ref, coup_ref, arrow_ref, *refs):
    outs, sems = refs[:-1], refs[-1]
    share, nodes = diag_ref.shape[1:]
    effects = arrow_ref.shape[1]
    member = where_ref[0]
    own_at = pl.multiple_of(member * share, share)
    other_at = pl.multiple_of((1 - member) * share, share)
    copies = []
    for n, out in enumerate(outs):
        pairs = [(diag_ref.at[1, :, pl.ds(own_at + n * PANEL, PANEL)], out.at[pl.ds(0, share)])]
        for c in range(0, share, PANEL):
            pairs.append(
                (coup_ref.at[0, pl.ds(n * PANEL, PANEL), pl.ds(other_at + c, PANEL)], out.at[pl.ds(share + c, PANEL)])
            )
        for m in range(2):
            source = arrow_ref.at[1, :, pl.ds(m * share + n * PANEL, PANEL)]
            pairs.append((source, out.at[pl.ds(nodes + m * effects, effects)]))
        for source, target in pairs:
            copies.append(pltpu.make_async_copy(source, target, sems.at[len(copies)]))
    for copy in copies:
        copy.start()
    for copy in copies:
        copy.wait()


def exchange(member, diag_block, coupling, arrow):
    share, nodes = diag_block.shape[1:]
    effects = arrow.shape[1]
    count = share // PANEL
    rows = nodes + 2 * effects
    anywhere = pl.BlockSpec(memory_space=pl.ANY)
    return pl.pallas_call(
        exchange_kernel,
        out_shape=[jax.ShapeDtypeStruct((rows, PANEL), jnp.float32)] * count,
        in_specs=[pl.BlockSpec(memory_space=pltpu.SMEM)] + [anywhere] * 3,
        out_specs=[pl.BlockSpec(memory_space=pltpu.VMEM)] * count,
        scratch_shapes=[pltpu.SemaphoreType.DMA((count * (3 + count),))],
        compiler_params=pltpu.CompilerParams(vmem_limit_bytes=56 * 1024 * 1024),
        cost_estimate=SMALL,
        name="exchange",
    )(member, diag_block, coupling, arrow)


def own_products_kernel(half, count, share, effects, skipped, *refs):
    where_ref, diag_ref, arrow_ref = refs[:3]
    highs, lows, refs = refs[3 : 3 + count], refs[3 + count : 3 + 2 * count], refs[3 + 2 * count :]
    if half:
        crosses, refs = refs[:count], refs[count:]
    refs = refs[skipped:]
    pivot_ref, right_ref, arrow_out_ref = refs[:3]
    high, low, other, pivot, middle, lines, sems, out_sems = refs[3:]
    member = where_ref[0]
    rows = 2 * share + effects
    columns = pl.ds(pl.multiple_of((1 - member if half else member) * share, share), share)
    copies = []
    for n in range(count):
        skip = highs[n].shape[0] - rows - effects
        copies.append(pltpu.make_async_copy(highs[n].at[pl.ds(skip, rows)], high.at[:, pl.ds(n * PANEL, PANEL)], sems.at[3 * n]))
        copies.append(pltpu.make_async_copy(lows[n].at[pl.ds(skip, rows)], low.at[:, pl.ds(n * PANEL, PANEL)], sems.at[3 * n + 1]))
        if half:
            copies.append(pltpu.make_async_copy(crosses[n], other.at[:, pl.ds(n * PANEL, PANEL)], sems.at[3 * n + 2]))
    copies.append(pltpu.make_async_copy(diag_ref.at[0, :, columns], pivot, sems.at[3 * count]))
    copies.append(pltpu.make_async_copy(arrow_ref.at[0, :, columns], lines, sems.at[3 * count + 1]))
    for copy in copies:
        copy.start()
    for copy in copies:
        copy.wait()
    for c in range(0, share, PANEL):
        if half:
            right = right_terms(*split(other[c : c + PANEL, :]))
        else:
            right = right_terms(high[share + c : share + c + PANEL, :], low[share + c : share + c + PANEL, :])
        for at, size in spans(0, rows, PANEL):
            value = plain_nt(left_terms(high[at : at + size, :], low[at : at + size, :]), right)
            if at < share:
                middle[at : at + size, c : c + PANEL] = -value
            elif at < 2 * share:
                to = at - share
                pivot[to : to + size, c : c + PANEL] = pivot[to : to + size, c : c + PANEL] - value
            else:
                lines[:, c : c + PANEL] = lines[:, c : c + PANEL] - value
    results = [
        (pivot, pivot_ref.at[:, columns]), (middle, right_ref.at[0, :, columns]), (lines, arrow_out_ref.at[:, columns])
    ]
    results = [pltpu.make_async_copy(source, target, out_sems.at[n]) for n, (source, target) in enumerate(results)]
    for copy in results:
        copy.start()
    for copy in results:
        copy.wait()


def own_products(half, member, diag_block, arrow, highs, lows, crosses, before):
    share, nodes = diag_block.shape[1:]
    effects = arrow.shape[1]
    count = len(highs)
    rows = 2 * share + effects
    anywhere = pl.BlockSpec(memory_space=pl.ANY)
    scalar = pl.BlockSpec(memory_space=pltpu.SMEM)
    shapes = [(share, nodes), (1, share, nodes), (effects, nodes)]
    operands = [member, diag_block, arrow, *highs, *lows, *crosses]
    aliases = {len(operands) + n: n for n in range(len(before))}
    operands += before
    return pl.pallas_call(
        functools.partial(own_products_kernel, half, count, share, effects, len(before)),
        out_shape=[jax.ShapeDtypeStruct(shape, jnp.float32) for shape in shapes],
        in_specs=[scalar] + [anywhere] * (len(operands) - 1),
        out_specs=[anywhere] * 3,
        scratch_shapes=[
            pltpu.VMEM((rows, nodes), jnp.bfloat16),
            pltpu.VMEM((rows, nodes), jnp.bfloat16),
            pltpu.VMEM((share, nodes), jnp.float32),
            pltpu.VMEM((share, share), jnp.float32),
            pltpu.VMEM((share, share), jnp.float32),
            pltpu.VMEM((effects, share), jnp.float32),
            pltpu.SemaphoreType.DMA((3 * count + 2,)),
            pltpu.SemaphoreType.DMA((3,)),
        ],
        input_output_aliases=aliases,
        compiler_params=pltpu.CompilerParams(vmem_limit_bytes=40 * 1024 * 1024),
        cost_estimate=SMALL,
        name=f"own_products_{half}",
    )(*operands)


def next_products_kernel(count, with_left, share, effects, *refs):
    where_ref, pivot_in, arrow_in = refs[:3]
    refs = refs[3:]
    if with_left:
        left_in, refs = refs[0], refs[1:]
    owns, others = refs[:count], refs[count : 2 * count]
    refs = refs[2 * count :]
    pivot_ref, left_ref, arrow_ref = refs[:3]
    own, other, pivot, middle, lines, sems, out_sems = refs[3:]
    member = where_ref[0]
    rows = 2 * share + effects
    copies = []
    for n in range(count):
        copies.append(pltpu.make_async_copy(owns[n], own.at[:, pl.ds(n * PANEL, PANEL)], sems.at[2 * n]))
        copies.append(pltpu.make_async_copy(others[n], other.at[:, pl.ds(n * PANEL, PANEL)], sems.at[2 * n + 1]))
    copies.append(pltpu.make_async_copy(pivot_in, pivot, sems.at[2 * count]))
    copies.append(pltpu.make_async_copy(arrow_in, lines, sems.at[2 * count + 1]))
    if with_left:
        copies.append(pltpu.make_async_copy(left_in, middle, sems.at[2 * count + 2]))
    for copy in copies:
        copy.start()
    for copy in copies:
        copy.wait()
    own_at = pl.multiple_of(member * share, share)
    other_at = pl.multiple_of((1 - member) * share, share)
    right = [
        [right_terms(*split(source[c : c + PANEL, :])) for c in range(0, share, PANEL)] for source in (own, other)
    ]
    for at, size in spans(0, rows, PANEL):
        left = left_terms(*split(own[at : at + size, :]))
        for half, base in ((0, own_at), (1, other_at)):
            for c in range(0, share, PANEL):
                columns = pl.ds(pl.multiple_of(base + c, PANEL), PANEL)
                value = plain_nt(left, right[half][c // PANEL])
                if at < share:
                    pivot[at : at + size, columns] = pivot[at : at + size, columns] - value
                elif at < 2 * share:
                    to = at - share
                    if with_left:
                        middle[to : to + size, columns] = middle[to : to + size, columns] - value
                    else:
                        middle[to : to + size, columns] = -value
                else:
                    lines[:, columns] = lines[:, columns] - value
    results = [(pivot, pivot_ref), (middle, left_ref), (lines, arrow_ref)]
    results = [pltpu.make_async_copy(source, target, out_sems.at[n]) for n, (source, target) in enumerate(results)]
    for copy in results:
        copy.start()
    for copy in results:
        copy.wait()


def next_products(member, pivot, arrow, left, owns, others):
    share, nodes = pivot.shape
    effects = arrow.shape[0]
    count = len(owns)
    rows = 2 * share + effects
    anywhere = pl.BlockSpec(memory_space=pl.ANY)
    scalar = pl.BlockSpec(memory_space=pltpu.SMEM)
    with_left = left is not None
    operands = [member, pivot, arrow] + ([left] if with_left else []) + [*owns, *others]
    shapes = [(share, nodes), (share, nodes), (effects, nodes)]
    return pl.pallas_call(
        functools.partial(next_products_kernel, count, with_left, share, effects),
        out_shape=[jax.ShapeDtypeStruct(shape, jnp.float32) for shape in shapes],
        in_specs=[scalar] + [anywhere] * (len(operands) - 1),
        out_specs=[anywhere] * 3,
        scratch_shapes=[
            pltpu.VMEM((rows, count * PANEL), jnp.float32),
            pltpu.VMEM((share, count * PANEL), jnp.float32),
            pltpu.VMEM((share, nodes), jnp.float32),
            pltpu.VMEM((share, nodes), jnp.float32),
            pltpu.VMEM((effects, nodes), jnp.float32),
            pltpu.SemaphoreType.DMA((2 * count + 3,)),
            pltpu.SemaphoreType.DMA((3,)),
        ],
        compiler_params=pltpu.CompilerParams(vmem_limit_bytes=24 * 1024 * 1024),
        cost_estimate=SMALL,
        name=f"next_products_{count}",
    )(*operands)


def local(diag_block, coupling, arrow, corner):
    partition_count = lax.axis_size("tm")
    position = lax.axis_index("tm")
    at = lax.axis_index("blk").astype(jnp.int32)
    member = at.reshape((1,))
    opened = (position < partition_count - 1).astype(jnp.int32).reshape((1,))
    share, nodes = diag_block.shape[1:]
    halves = [swapped(part) for part in exchange(member, diag_block, coupling, arrow)]
    earlier, results, highs, lows, crosses, owns, others = [], [], [], [], [], [], []
    for index in range(nodes // PANEL):
        inputs = (member, opened, diag_block, coupling, arrow, halves[index % len(halves)])
        order = []
        if index > 1:
            order = [owns[index - 2], crosses[index - 2], *others[index - 3 : index - 2]]
        found = panel(index, inputs, earlier, results, order)
        results = found[:4]
        send, cross, high, low = found[4:8]
        earlier += [high, low]
        highs.append(high)
        lows.append(low)
        owns.append(shifted(send, "tm", 1))
        crosses.append(swapped(cross))
        if index < nodes // PANEL - 2:
            others.append(swapped(owns[-1][:share]))
    sums = corner_rounds(partition_count)
    total = found[8] if sums else lax.psum(found[8], "tm")
    products = own_products(0, member, diag_block, arrow, highs, lows, [], [])
    products = own_products(1, member, diag_block, arrow, highs, lows, crosses, products)
    pivot, right_out, lines = products
    before = after(owns[-2], products[0])
    others.append(swapped(before[:share]))
    pivot, left, lines = next_products(member, pivot, lines, None, [*owns[:-2], before], others)
    for steps, size in sums[:-1]:
        total = grouped_sum(total, "tm", steps, size, pivot)
    final = after(owns[-1], pivot)
    pivot, left, lines = next_products(member, pivot, lines, left, [final], [swapped(final[:share])])
    for steps, size in sums[-1:]:
        total = grouped_sum(total, "tm", steps, size, pivot)
    corner_out = corner - total
    return (*results, pivot[None], left[None], right_out, lines[None], corner_out)


def solution(mesh):
    placed = (P("tm", "blk", None), P("tm", "blk", None), P("tm", "blk", None), P("blk", None))
    return jax.shard_map(
        local,
        mesh=mesh,
        in_specs=placed,
        out_specs=(P("tm", "blk", None),) * 8 + (P("blk", None),),
        check_vma=False,
    )
```

```python
import functools

import jax
import jax.numpy as jnp
from jax import lax
from jax.experimental import pallas as pl
from jax.experimental.pallas import tpu as pltpu
from jax.sharding import PartitionSpec as P

BLOCK = 128
PANEL = 256
SMALL = pl.CostEstimate(flops=10**6, bytes_accessed=10**4, transcendentals=0)


def shifted(value, axis, steps):
    count = lax.axis_size(axis)
    leading, last = (max(0, -steps), min(count, count - steps))
    return lax.ppermute(value, axis, [(source, source + steps) for source in range(leading, last)])


def swapped(value):
    return lax.ppermute(value, "blk", [(0, 1), (1, 0)])


def after(value, *earlier):
    return lax.optimization_barrier((value, *earlier))[0]


def corner_rounds(count):
    rounds, steps = [], 1
    while count % 2 == 0:
        size = 4 if count % 4 == 0 else 2
        rounds.append((steps, size))
        steps, count = steps * size, count // size
    return rounds if count == 1 else []


def grouped_sum(value, axis, steps, size, *earlier):
    count = lax.axis_size(axis)
    found = [
        lax.ppermute(value, axis, [(source, source ^ (other * steps)) for source in range(count)])
        for other in range(1, size)
    ]
    found = lax.optimization_barrier((*found, *earlier))[: size - 1]
    value = value + found[0]
    return value + (found[1] + found[2]) if size == 4 else value


def exact(left, right, right_dim):
    return lax.dot_general(
        left, right, (((1,), (right_dim,)), ((), ())), precision=lax.Precision.HIGHEST, preferred_element_type=jnp.float32
    )


def plain_nt(left, right):
    return lax.dot_general(left, right, (((1,), (1,)), ((), ())), preferred_element_type=jnp.float32)


def split(value):
    high = value.astype(jnp.bfloat16)
    low = (value - high.astype(jnp.float32)).astype(jnp.bfloat16)
    return high, low


def left_terms(high, low):
    return jnp.concatenate([high, low, high], axis=1)


def right_terms(high, low):
    return jnp.concatenate([high, high, low], axis=1)


def inverse_of_factor(block, tasks):
    shape = (8, BLOCK)
    lane = lax.broadcasted_iota(jnp.int32, shape, 1)
    sub = lax.broadcasted_iota(jnp.int32, shape, 0)

    def along_lanes(value, at):
        return jnp.broadcast_to(value[:, at : at + 1], shape)

    def along_rows(value, at):
        return jnp.broadcast_to(value[at : at + 1, :], shape)

    groups = BLOCK // 8
    rows = [block[8 * g : 8 * g + 8, :] for g in range(groups)]
    done = []
    for b in range(groups):
        k = 8 * b
        own = rows[b]
        inside = (lane >= k) & (lane < k + 8)
        columns = [along_lanes(own, k + j) for j in range(8)]
        entry = {(i, j): along_rows(columns[j], i) for j in range(8) for i in range(j, 8)}
        unit = jnp.where(inside, (lane - k == sub).astype(jnp.float32), own)
        line = [along_rows(unit, i) for i in range(8)]
        last = b == groups - 1
        if not last:
            following = rows[b + 1]
            mults = [along_lanes(following, k + j) for j in range(8)]
            following = jnp.where(inside, 0.0, following)
        rows_of, solved = [None] * 8, [None] * 8
        pivots = []
        for j in range(0, 8, 2):
            p, q, s = entry[j, j], entry[j + 1, j], entry[j + 1, j + 1]
            root = lax.rsqrt(p * s - q * q)
            over = root * root
            pivots.append((p, q, s, over))
            for m in range(j + 2, 8):
                at_first = s * entry[m, j] - q * entry[m, j + 1]
                at_second = p * entry[m, j + 1] - q * entry[m, j]
                for i in range(m, 8):
                    entry[i, m] = entry[i, m] - (entry[i, j] * at_first + entry[i, j + 1] * at_second) * over
            solved[j] = (s * line[j] - q * line[j + 1]) * over
            solved[j + 1] = (p * line[j + 1] - q * line[j]) * over
            for i in range(j + 2, 8):
                line[i] = line[i] - (entry[i, j] * solved[j] + entry[i, j + 1] * solved[j + 1])
            if not last:
                following = following - (mults[j] * solved[j] + mults[j + 1] * solved[j + 1])
                if j < 6:
                    at_first = (s * mults[j] - q * mults[j + 1]) * over
                    at_second = (p * mults[j + 1] - q * mults[j]) * over
                    for i in range(j + 2, 8):
                        mults[i] = mults[i] - (entry[i, j] * at_first + entry[i, j + 1] * at_second)
            first_scale = lax.rsqrt(p)
            rows_of[j] = line[j] * first_scale
            rows_of[j + 1] = (line[j + 1] - (q * first_scale) * rows_of[j]) * (root * (p * first_scale))
        compact = rows_of[0]
        for j in range(1, 8):
            compact = jnp.where(sub == j, rows_of[j], compact)
        done.append(jnp.where(lane <= k + sub, compact, 0.0))
        if not last:
            rows[b + 1] = following
        if b + 2 < groups:
            for j in range(4, -1, -2):
                p, q, s, over = pivots[j // 2]
                first, second = entry[j + 2, j] * solved[j + 2], entry[j + 2, j + 1] * solved[j + 2]
                for i in range(j + 3, 8):
                    first = first + entry[i, j] * solved[i]
                    second = second + entry[i, j + 1] * solved[i]
                solved[j] = solved[j] - (s * first - q * second) * over
                solved[j + 1] = solved[j + 1] - (p * second - q * first) * over
            for g in range(b + 2, groups):
                target = rows[g]
                left = [along_lanes(target, k + j) for j in range(8)]
                target = jnp.where(inside, 0.0, target)
                for j in range(0, 8, 2):
                    target = target - (left[j] * solved[j] + left[j + 1] * solved[j + 1])
                rows[g] = target
        for task in tasks[b]:
            task()
    return jnp.concatenate(done, axis=0)


def spans(start, stop, size):
    return [(at, min(size, stop - at)) for at in range(start, stop, size)]


def panel_kernel(index, count, share, effects, skipped, *refs):
    nodes = 2 * share
    last = index == count - 1
    inputs, refs = refs[: 6 + 2 * index], refs[6 + 2 * index :]
    where_ref, open_ref, diag_ref, coup_ref, arrow_ref, other_ref = inputs[:6]
    earlier = inputs[6:]
    refs = refs[skipped:]
    factor_ref, first_ref, second_ref, third_ref, send_ref, cross_ref, high_ref, low_ref = refs[:8]
    if last:
        corner_ref = refs[8]
    work, stage, turned, factor, high, low, high_before, low_before, sems, before_sems, out_sems = refs[8 + last :]
    member = where_ref[0]
    start = index * PANEL
    square = nodes - start
    total = square + 2 * share + 2 * effects
    columns = pl.ds(start, PANEL)
    second_at, first_at, third_at = square, square + share, square + 2 * share

    holder, inner = divmod(start, share)
    held = share - inner
    rest = square - held

    def split_copies(owner):
        if owner == holder:
            pairs = [
                (diag_ref.at[1, pl.ds(inner, held), columns], work.at[pl.ds(0, held)]),
                (coup_ref.at[0, pl.ds(inner, PANEL), pl.ds(owner * share, share)], stage),
            ]
            if rest:
                pairs.append((diag_ref.at[1, pl.ds(inner, PANEL), pl.ds(share, share)], turned))
        else:
            pairs = [(other_ref.at[pl.ds(inner, held)], work.at[pl.ds(0, held)])]
            for c in range(0, share, PANEL):
                pairs.append((other_ref.at[pl.ds(share + c, PANEL)], stage.at[:, pl.ds(c, PANEL)]))
            if rest:
                pairs.append((diag_ref.at[1, :, columns], work.at[pl.ds(held, rest)]))
        return [pltpu.make_async_copy(*pair, sems.at[n]) for n, pair in enumerate(pairs)]

    for owner in range(2):
        @pl.when(member == owner)
        def _():
            for copy in split_copies(owner):
                copy.start()

    same = [
        pltpu.make_async_copy(coup_ref.at[1, :, columns], work.at[pl.ds(second_at, share)], sems.at[4]),
        pltpu.make_async_copy(arrow_ref.at[1, :, columns], work.at[pl.ds(third_at, effects)], sems.at[5]),
        pltpu.make_async_copy(
            other_ref.at[pl.ds(nodes + holder * effects, effects)], work.at[pl.ds(third_at + effects, effects)], sems.at[6]
        ),
    ]
    first = []
    for j in range(index):
        skip = start - j * PANEL
        for n, (source, target) in enumerate(((earlier[2 * j], high_before), (earlier[2 * j + 1], low_before))):
            for copies, at, size in ((first, 0, PANEL), (same, PANEL, total - PANEL)):
                sem = before_sems.at[4 * j + 2 * n + (at > 0)]
                copies.append(
                    pltpu.make_async_copy(source.at[pl.ds(skip + at, size)], target.at[j, pl.ds(at, size)], sem)
                )
    for copy in first + same:
        copy.start()
    if start:
        factor[0:start, :] = jnp.zeros((start, PANEL), jnp.float32)
    def update(at, size):
        if not index:
            return
        value = work[at : at + size, :]
        for j in range(index):
            left = left_terms(high_before[j, at : at + size, :], low_before[j, at : at + size, :])
            right = right_terms(high_before[j, 0:PANEL, :], low_before[j, 0:PANEL, :])
            value = value - plain_nt(left, right)
        work[at : at + size, :] = value

    split_copies(0)[0].wait()
    for copy in first:
        copy.wait()
    update(0, PANEL)
    for owner in range(2):
        @pl.when(member == owner)
        def _():
            for copy in split_copies(owner)[1:]:
                copy.wait()
            if owner == holder and rest:
                for r in range(0, PANEL, BLOCK):
                    for c in range(0, rest, BLOCK):
                        work[held + c : held + c + BLOCK, r : r + BLOCK] = turned[r : r + BLOCK, c : c + BLOCK].T

    for copy in same:
        copy.wait()

    @pl.when(open_ref[0] == 0)
    def _():
        work[second_at : second_at + share, :] = jnp.zeros((share, PANEL), jnp.float32)

    for r in range(0, PANEL, BLOCK):
        for c in range(0, share, BLOCK):
            work[first_at + c : first_at + c + BLOCK, r : r + BLOCK] = stage[r : r + BLOCK, c : c + BLOCK].T

    waiting = spans(PANEL, total, BLOCK)
    tasks = [[] for _ in range(32)]
    for n, (at, size) in enumerate(waiting):
        tasks[(32 * n) // len(waiting)].append(functools.partial(update, at, size))

    head = work[0:BLOCK, 0:BLOCK]
    side = work[BLOCK:PANEL, 0:BLOCK]
    tail = work[BLOCK:PANEL, BLOCK:PANEL]
    head_inverse = inverse_of_factor(head, tasks[:16])
    beside = exact(side, head_inverse, 1)
    across = exact(beside, head_inverse, 0)
    tail_inverse = inverse_of_factor(tail - exact(beside, beside, 1), tasks[16:])
    corner = -exact(tail_inverse, across, 0)
    inverse = jnp.concatenate(
        [
            jnp.concatenate([head_inverse, jnp.zeros((BLOCK, BLOCK), jnp.float32)], axis=1),
            jnp.concatenate([corner, tail_inverse], axis=1),
        ],
        axis=0,
    )
    right = right_terms(*split(inverse))

    def solve(at, size):
        solved = plain_nt(left_terms(*split(work[at : at + size, :])), right)
        if at < PANEL:
            row = lax.broadcasted_iota(jnp.int32, solved.shape, 0) + at
            lane = lax.broadcasted_iota(jnp.int32, solved.shape, 1)
            solved = jnp.where(row >= lane, solved, 0.0)
        if at < square:
            factor[start + at : start + at + size, :] = solved
        else:
            work[at : at + size, :] = solved
        high[at : at + size, :], low[at : at + size, :] = split(solved)

    sends = [
        (work.at[pl.ds(second_at, 2 * share + effects)], send_ref),
        (work.at[pl.ds(first_at, share)], cross_ref),
        (work.at[pl.ds(first_at, share)], first_ref.at[0, :, columns]),
        (work.at[pl.ds(second_at, share)], second_ref.at[0, :, columns]),
        (work.at[pl.ds(third_at, effects)], third_ref.at[0, :, columns]),
        (factor.at[pl.ds(pl.multiple_of(member * share, share), share)], factor_ref.at[0, :, columns]),
        (high, high_ref),
        (low, low_ref),
    ]
    sends = [pltpu.make_async_copy(source, target, out_sems.at[n]) for n, (source, target) in enumerate(sends)]
    for at, size in spans(square, total, PANEL):
        solve(at, size)
    for copy in sends[:5]:
        copy.start()
    for at, size in spans(0, square, PANEL):
        solve(at, size)
    for copy in sends[5:]:
        copy.start()
    if last:
        at, size = third_at, 2 * effects
        value = plain_nt(
            left_terms(high[at : at + effects, :], low[at : at + effects, :]),
            right_terms(high[at : at + size, :], low[at : at + size, :]),
        )
        for j in range(index):
            value = value + plain_nt(
                left_terms(high_before[j, at : at + effects, :], low_before[j, at : at + effects, :]),
                right_terms(high_before[j, at : at + size, :], low_before[j, at : at + size, :]),
            )
        crossed = jnp.concatenate([value[:, effects:], value[:, :effects]], axis=1)
        corner_ref[...] = jnp.where(member == 0, value, crossed)
    for copy in sends:
        copy.wait()


def panel(index, inputs, earlier, results, order):
    member, opened, diag_block, coupling, arrow, other = inputs
    share, nodes = diag_block.shape[1:]
    effects = arrow.shape[1]
    count = nodes // PANEL
    total = nodes - index * PANEL + 2 * share + 2 * effects
    anywhere = pl.BlockSpec(memory_space=pl.ANY)
    scalar = pl.BlockSpec(memory_space=pltpu.SMEM)
    pinned = pl.BlockSpec(memory_space=pltpu.HBM)
    whole = pl.BlockSpec(memory_space=pltpu.VMEM)
    shapes = [
        ((1, share, nodes), jnp.float32), ((1, share, nodes), jnp.float32),
        ((1, share, nodes), jnp.float32), ((1, effects, nodes), jnp.float32),
        ((2 * share + effects, PANEL), jnp.float32), ((share, PANEL), jnp.float32),
        ((total, PANEL), jnp.bfloat16), ((total, PANEL), jnp.bfloat16),
    ]
    outs = [anywhere] * len(shapes)
    if index == count - 1:
        shapes.append(((effects, 2 * effects), jnp.float32))
        outs.append(pl.BlockSpec(memory_space=pltpu.VMEM))
    operands = [*inputs, *earlier, *results, *order]
    aliases = {6 + len(earlier) + n: n for n in range(len(results))}
    return pl.pallas_call(
        functools.partial(panel_kernel, index, count, share, effects, len(results) + len(order)),
        out_shape=[jax.ShapeDtypeStruct(shape, kind) for shape, kind in shapes],
        in_specs=[scalar, scalar, *[pinned] * 3, anywhere if index else whole, *[anywhere] * (len(operands) - 6)],
        out_specs=outs,
        scratch_shapes=[
            pltpu.VMEM((total, PANEL), jnp.float32),
            pltpu.VMEM((PANEL, share), jnp.float32),
            pltpu.VMEM((PANEL, share), jnp.float32),
            pltpu.VMEM((nodes, PANEL), jnp.float32),
            pltpu.VMEM((total, PANEL), jnp.bfloat16),
            pltpu.VMEM((total, PANEL), jnp.bfloat16),
            pltpu.VMEM((max(index, 1), total, PANEL), jnp.bfloat16),
            pltpu.VMEM((max(index, 1), total, PANEL), jnp.bfloat16),
            pltpu.SemaphoreType.DMA((7,)),
            pltpu.SemaphoreType.DMA((max(4 * index, 1),)),
            pltpu.SemaphoreType.DMA((8,)),
        ],
        input_output_aliases=aliases,
        compiler_params=pltpu.CompilerParams(vmem_limit_bytes=(40 if index else 56) * 1024 * 1024),
        cost_estimate=SMALL,
        name=f"panel_{index}",
    )(*operands)


def exchange_kernel(n, where_ref, diag_ref, coup_ref, arrow_ref, out, sems):
    share, nodes = diag_ref.shape[1:]
    effects = arrow_ref.shape[1]
    member = where_ref[0]
    own_at = pl.multiple_of(member * share, share)
    other_at = pl.multiple_of((1 - member) * share, share)
    pairs = [(diag_ref.at[1, :, pl.ds(own_at + n * PANEL, PANEL)], out.at[pl.ds(0, share)])]
    for c in range(0, share, PANEL):
        pairs.append(
            (coup_ref.at[0, pl.ds(n * PANEL, PANEL), pl.ds(other_at + c, PANEL)], out.at[pl.ds(share + c, PANEL)])
        )
    for m in range(2):
        source = arrow_ref.at[1, :, pl.ds(m * share + n * PANEL, PANEL)]
        pairs.append((source, out.at[pl.ds(nodes + m * effects, effects)]))
    copies = [pltpu.make_async_copy(*pair, sems.at[at]) for at, pair in enumerate(pairs)]
    for copy in copies:
        copy.start()
    for copy in copies:
        copy.wait()


def exchange(n, member, diag_block, coupling, arrow):
    share, nodes = diag_block.shape[1:]
    effects = arrow.shape[1]
    return pl.pallas_call(
        functools.partial(exchange_kernel, n),
        out_shape=jax.ShapeDtypeStruct((nodes + 2 * effects, PANEL), jnp.float32),
        in_specs=[pl.BlockSpec(memory_space=pltpu.SMEM)] + [pl.BlockSpec(memory_space=pltpu.HBM)] * 3,
        out_specs=pl.BlockSpec(memory_space=pltpu.VMEM),
        scratch_shapes=[pltpu.SemaphoreType.DMA((3 + share // PANEL,))],
        compiler_params=pltpu.CompilerParams(vmem_limit_bytes=56 * 1024 * 1024),
        cost_estimate=SMALL,
        name=f"exchange_{n}",
    )(member, diag_block, coupling, arrow)


def own_products_kernel(half, count, share, effects, skipped, *refs):
    where_ref, diag_ref, arrow_ref = refs[:3]
    highs, lows, refs = refs[3 : 3 + count], refs[3 + count : 3 + 2 * count], refs[3 + 2 * count :]
    if half:
        crosses, refs = refs[:count], refs[count:]
    refs = refs[skipped:]
    pivot_ref, right_ref, arrow_out_ref = refs[:3]
    high, low, other, pivot, middle, lines, sems, out_sems = refs[3:]
    member = where_ref[0]
    rows = 2 * share + effects
    columns = pl.ds(pl.multiple_of((1 - member if half else member) * share, share), share)
    copies = []
    for n in range(count):
        skip = highs[n].shape[0] - rows - effects
        copies.append(pltpu.make_async_copy(highs[n].at[pl.ds(skip, rows)], high.at[:, pl.ds(n * PANEL, PANEL)], sems.at[3 * n]))
        copies.append(pltpu.make_async_copy(lows[n].at[pl.ds(skip, rows)], low.at[:, pl.ds(n * PANEL, PANEL)], sems.at[3 * n + 1]))
        if half:
            copies.append(pltpu.make_async_copy(crosses[n], other.at[:, pl.ds(n * PANEL, PANEL)], sems.at[3 * n + 2]))
    copies.append(pltpu.make_async_copy(diag_ref.at[0, :, columns], pivot, sems.at[3 * count]))
    copies.append(pltpu.make_async_copy(arrow_ref.at[0, :, columns], lines, sems.at[3 * count + 1]))
    for copy in copies:
        copy.start()
    for copy in copies:
        copy.wait()
    for c in range(0, share, PANEL):
        if half:
            right = right_terms(*split(other[c : c + PANEL, :]))
        else:
            right = right_terms(high[share + c : share + c + PANEL, :], low[share + c : share + c + PANEL, :])
        for at, size in spans(0, rows, PANEL):
            value = plain_nt(left_terms(high[at : at + size, :], low[at : at + size, :]), right)
            if at < share:
                middle[at : at + size, c : c + PANEL] = -value
            elif at < 2 * share:
                to = at - share
                pivot[to : to + size, c : c + PANEL] = pivot[to : to + size, c : c + PANEL] - value
            else:
                lines[:, c : c + PANEL] = lines[:, c : c + PANEL] - value
    results = [
        (pivot, pivot_ref.at[:, columns]), (middle, right_ref.at[0, :, columns]), (lines, arrow_out_ref.at[:, columns])
    ]
    results = [pltpu.make_async_copy(source, target, out_sems.at[n]) for n, (source, target) in enumerate(results)]
    for copy in results:
        copy.start()
    for copy in results:
        copy.wait()


def own_products(half, member, diag_block, arrow, highs, lows, crosses, before):
    share, nodes = diag_block.shape[1:]
    effects = arrow.shape[1]
    count = len(highs)
    rows = 2 * share + effects
    anywhere = pl.BlockSpec(memory_space=pl.ANY)
    scalar = pl.BlockSpec(memory_space=pltpu.SMEM)
    shapes = [(share, nodes), (1, share, nodes), (effects, nodes)]
    operands = [member, diag_block, arrow, *highs, *lows, *crosses]
    aliases = {len(operands) + n: n for n in range(len(before))}
    operands += before
    return pl.pallas_call(
        functools.partial(own_products_kernel, half, count, share, effects, len(before)),
        out_shape=[jax.ShapeDtypeStruct(shape, jnp.float32) for shape in shapes],
        in_specs=[scalar] + [pl.BlockSpec(memory_space=pltpu.HBM)] * 2 + [anywhere] * (len(operands) - 3),
        out_specs=[anywhere] * 3,
        scratch_shapes=[
            pltpu.VMEM((rows, nodes), jnp.bfloat16),
            pltpu.VMEM((rows, nodes), jnp.bfloat16),
            pltpu.VMEM((share, nodes), jnp.float32),
            pltpu.VMEM((share, share), jnp.float32),
            pltpu.VMEM((share, share), jnp.float32),
            pltpu.VMEM((effects, share), jnp.float32),
            pltpu.SemaphoreType.DMA((3 * count + 2,)),
            pltpu.SemaphoreType.DMA((3,)),
        ],
        input_output_aliases=aliases,
        compiler_params=pltpu.CompilerParams(vmem_limit_bytes=40 * 1024 * 1024),
        cost_estimate=SMALL,
        name=f"own_products_{half}",
    )(*operands)


def next_products_kernel(count, with_left, share, effects, *refs):
    where_ref, pivot_in, arrow_in = refs[:3]
    refs = refs[3:]
    if with_left:
        left_in, refs = refs[0], refs[1:]
    owns, others, refs = refs[:count], refs[count : 2 * count], refs[2 * count :]
    pivot_ref, left_ref, arrow_ref, pivot, middle, lines, sems = refs
    member = where_ref[0]
    rows = 2 * share + effects
    own_at = pl.multiple_of(member * share, share)
    other_at = pl.multiple_of((1 - member) * share, share)

    def across(parts, at, size):
        return split(jnp.concatenate([part[at : at + size, :] for part in parts], axis=1))

    right = [[right_terms(*across(parts, c, PANEL)) for c in range(0, share, PANEL)] for parts in (owns, others)]
    copies = []
    for at, size in spans(0, rows, PANEL):
        left = left_terms(*across(owns, at, size))
        to = at % share
        for half, base in ((0, own_at), (1, other_at)):
            for c in range(0, share, PANEL):
                columns = pl.ds(pl.multiple_of(base + c, PANEL), PANEL)
                value = plain_nt(left, right[half][c // PANEL])
                if at < share:
                    pivot[to : to + size, columns] = pivot_in[to : to + size, columns] - value
                elif at >= 2 * share:
                    lines[:, columns] = arrow_in[:, columns] - value
                elif with_left:
                    middle[to : to + size, columns] = left_in[to : to + size, columns] - value
                else:
                    middle[to : to + size, columns] = -value
        source, target = ((pivot, pivot_ref), (middle, left_ref), (lines, arrow_ref))[at // share]
        rows_here = pl.ds(to, size)
        copies.append(pltpu.make_async_copy(source.at[rows_here], target.at[rows_here], sems.at[len(copies)]))
        copies[-1].start()
    for copy in copies:
        copy.wait()


def next_products(member, pivot, arrow, left, owns, others):
    share, nodes = pivot.shape
    effects = arrow.shape[0]
    count = len(owns)
    rows = 2 * share + effects
    anywhere = pl.BlockSpec(memory_space=pl.ANY)
    scalar = pl.BlockSpec(memory_space=pltpu.SMEM)
    with_left = left is not None
    operands = [member, pivot, arrow] + ([left] if with_left else []) + [*owns, *others]
    shapes = [(share, nodes), (share, nodes), (effects, nodes)]
    return pl.pallas_call(
        functools.partial(next_products_kernel, count, with_left, share, effects),
        out_shape=[jax.ShapeDtypeStruct(shape, jnp.float32) for shape in shapes],
        in_specs=[scalar] + [pl.BlockSpec(memory_space=pltpu.VMEM)] * (len(operands) - 1),
        out_specs=[anywhere] * 3,
        scratch_shapes=[
            pltpu.VMEM((share, nodes), jnp.float32),
            pltpu.VMEM((share, nodes), jnp.float32),
            pltpu.VMEM((effects, nodes), jnp.float32),
            pltpu.SemaphoreType.DMA((len(spans(0, rows, PANEL)),)),
        ],
        compiler_params=pltpu.CompilerParams(vmem_limit_bytes=28 * 1024 * 1024),
        cost_estimate=SMALL,
        name=f"next_products_{count}",
    )(*operands)


def local(diag_block, coupling, arrow, corner):
    partition_count = lax.axis_size("tm")
    position = lax.axis_index("tm")
    at = lax.axis_index("blk").astype(jnp.int32)
    member = at.reshape((1,))
    opened = (position < partition_count - 1).astype(jnp.int32).reshape((1,))
    share, nodes = diag_block.shape[1:]
    halves = [swapped(exchange(n, member, diag_block, coupling, arrow)) for n in range(share // PANEL)]
    earlier, results, highs, lows, crosses, owns, others = [], [], [], [], [], [], []
    for index in range(nodes // PANEL):
        inputs = (member, opened, diag_block, coupling, arrow, halves[index % len(halves)])
        order = []
        if index > 1:
            order = [owns[index - 2], crosses[index - 2], *others[index - 3 : index - 2]]
        found = panel(index, inputs, earlier, results, order)
        results = found[:4]
        send, cross, high, low = found[4:8]
        earlier += [high, low]
        highs.append(high)
        lows.append(low)
        if index == nodes // PANEL - 1:
            sums = corner_rounds(partition_count)
            total = found[8] if sums else lax.psum(found[8], "tm")
            for steps, size in sums[:-1]:
                total = grouped_sum(total, "tm", steps, size)
            send = after(send, total)
        owns.append(shifted(send, "tm", 1))
        crosses.append(swapped(cross))
        if index < nodes // PANEL - 2:
            others.append(swapped(owns[-1][:share]))
    products = own_products(0, member, diag_block, arrow, highs, lows, [], [])
    products = own_products(1, member, diag_block, arrow, highs, lows, crosses, products)
    pivot, right_out, lines = products
    before = after(owns[-2], products[0])
    others.append(swapped(before[:share]))
    pivot, left, lines = next_products(member, pivot, lines, None, [*owns[:-2], before], others)
    final = after(owns[-1], pivot)
    pivot, left, lines = next_products(member, pivot, lines, left, [final], [swapped(final[:share])])
    for steps, size in sums[-1:]:
        total = grouped_sum(total, "tm", steps, size, pivot)
    corner_out = corner - total
    return (*results, pivot[None], left[None], right_out, lines[None], corner_out)


def solution(mesh):
    placed = (P("tm", "blk", None), P("tm", "blk", None), P("tm", "blk", None), P("blk", None))
    return jax.shard_map(
        local,
        mesh=mesh,
        in_specs=placed,
        out_specs=(P("tm", "blk", None),) * 8 + (P("blk", None),),
        check_vma=False,
    )
```

```python
import functools

import jax
import jax.numpy as jnp
from jax import lax
from jax.experimental import pallas as pl
from jax.experimental.pallas import tpu as pltpu
from jax.sharding import PartitionSpec as P

BLOCK = 128
PANEL = 256
SMALL = pl.CostEstimate(flops=10**6, bytes_accessed=10**4, transcendentals=0)


def shifted(value, axis, steps):
    count = lax.axis_size(axis)
    leading, last = (max(0, -steps), min(count, count - steps))
    return lax.ppermute(value, axis, [(source, source + steps) for source in range(leading, last)])


def swapped(value):
    return lax.ppermute(value, "blk", [(0, 1), (1, 0)])


def after(value, *earlier):
    return lax.optimization_barrier((value, *earlier))[0]


def corner_rounds(count):
    rounds, steps = [], 1
    while count % 2 == 0:
        size = 4 if count % 4 == 0 else 2
        rounds.append((steps, size))
        steps, count = steps * size, count // size
    return rounds if count == 1 else []


def grouped_sum(value, axis, steps, size, *earlier):
    count = lax.axis_size(axis)
    found = [
        lax.ppermute(value, axis, [(source, source ^ (other * steps)) for source in range(count)])
        for other in range(1, size)
    ]
    found = lax.optimization_barrier((*found, *earlier))[: size - 1]
    value = value + found[0]
    return value + (found[1] + found[2]) if size == 4 else value


def exact(left, right, right_dim):
    return lax.dot_general(
        left, right, (((1,), (right_dim,)), ((), ())), precision=lax.Precision.HIGHEST, preferred_element_type=jnp.float32
    )


def plain_nt(left, right):
    return lax.dot_general(left, right, (((1,), (1,)), ((), ())), preferred_element_type=jnp.float32)


def split(value):
    high = value.astype(jnp.bfloat16)
    low = (value - high.astype(jnp.float32)).astype(jnp.bfloat16)
    return high, low


def left_terms(high, low):
    return jnp.concatenate([high, low, high], axis=1)


def right_terms(high, low):
    return jnp.concatenate([high, high, low], axis=1)


def inverse_of_factor(block, tasks):
    shape = (8, BLOCK)
    lane = lax.broadcasted_iota(jnp.int32, shape, 1)
    sub = lax.broadcasted_iota(jnp.int32, shape, 0)

    def along_lanes(value, at):
        return jnp.broadcast_to(value[:, at : at + 1], shape)

    def along_rows(value, at):
        return jnp.broadcast_to(value[at : at + 1, :], shape)

    groups = BLOCK // 8
    rows = [block[8 * g : 8 * g + 8, :] for g in range(groups)]
    done = []
    for b in range(groups):
        k = 8 * b
        own = rows[b]
        inside = (lane >= k) & (lane < k + 8)
        columns = [along_lanes(own, k + j) for j in range(8)]
        entry = {(i, j): along_rows(columns[j], i) for j in range(8) for i in range(j, 8)}
        unit = jnp.where(inside, (lane - k == sub).astype(jnp.float32), own)
        line = [along_rows(unit, i) for i in range(8)]
        last = b == groups - 1
        if not last:
            following = rows[b + 1]
            mults = [along_lanes(following, k + j) for j in range(8)]
            following = jnp.where(inside, 0.0, following)
        rows_of, solved = [None] * 8, [None] * 8
        pivots = []
        for j in range(0, 8, 2):
            p, q, s = entry[j, j], entry[j + 1, j], entry[j + 1, j + 1]
            root = lax.rsqrt(p * s - q * q)
            over = root * root
            pivots.append((p, q, s, over))
            for m in range(j + 2, 8):
                at_first = s * entry[m, j] - q * entry[m, j + 1]
                at_second = p * entry[m, j + 1] - q * entry[m, j]
                for i in range(m, 8):
                    entry[i, m] = entry[i, m] - (entry[i, j] * at_first + entry[i, j + 1] * at_second) * over
            solved[j] = (s * line[j] - q * line[j + 1]) * over
            solved[j + 1] = (p * line[j + 1] - q * line[j]) * over
            for i in range(j + 2, 8):
                line[i] = line[i] - (entry[i, j] * solved[j] + entry[i, j + 1] * solved[j + 1])
            if not last:
                following = following - (mults[j] * solved[j] + mults[j + 1] * solved[j + 1])
                if j < 6:
                    at_first = (s * mults[j] - q * mults[j + 1]) * over
                    at_second = (p * mults[j + 1] - q * mults[j]) * over
                    for i in range(j + 2, 8):
                        mults[i] = mults[i] - (entry[i, j] * at_first + entry[i, j + 1] * at_second)
            first_scale = lax.rsqrt(p)
            rows_of[j] = line[j] * first_scale
            rows_of[j + 1] = (line[j + 1] - (q * first_scale) * rows_of[j]) * (root * (p * first_scale))
        compact = rows_of[0]
        for j in range(1, 8):
            compact = jnp.where(sub == j, rows_of[j], compact)
        done.append(jnp.where(lane <= k + sub, compact, 0.0))
        if not last:
            rows[b + 1] = following
        if b + 2 < groups:
            for j in range(4, -1, -2):
                p, q, s, over = pivots[j // 2]
                first, second = entry[j + 2, j] * solved[j + 2], entry[j + 2, j + 1] * solved[j + 2]
                for i in range(j + 3, 8):
                    first = first + entry[i, j] * solved[i]
                    second = second + entry[i, j + 1] * solved[i]
                solved[j] = solved[j] - (s * first - q * second) * over
                solved[j + 1] = solved[j + 1] - (p * second - q * first) * over
            for g in range(b + 2, groups):
                target = rows[g]
                left = [along_lanes(target, k + j) for j in range(8)]
                target = jnp.where(inside, 0.0, target)
                for j in range(0, 8, 2):
                    target = target - (left[j] * solved[j] + left[j + 1] * solved[j + 1])
                rows[g] = target
        for task in tasks[b]:
            task()
    return jnp.concatenate(done, axis=0)


def spans(start, stop, size):
    return [(at, min(size, stop - at)) for at in range(start, stop, size)]


def panel_kernel(index, count, share, effects, skipped, *refs):
    nodes = 2 * share
    last = index == count - 1
    inputs, refs = refs[: 6 + 2 * index], refs[6 + 2 * index :]
    where_ref, open_ref, diag_ref, coup_ref, arrow_ref, other_ref = inputs[:6]
    earlier = inputs[6:]
    refs = refs[skipped:]
    factor_ref, first_ref, second_ref, third_ref, send_ref, cross_ref, high_ref, low_ref = refs[:8]
    if last:
        corner_ref = refs[8]
    work, stage, turned, factor, high, low, high_before, low_before, sems, before_sems, out_sems = refs[8 + last :]
    member = where_ref[0]
    start = index * PANEL
    square = nodes - start
    total = square + 2 * share + 2 * effects
    columns = pl.ds(start, PANEL)
    second_at, first_at, third_at = square, square + share, square + 2 * share

    holder, inner = divmod(start, share)
    held = share - inner
    rest = square - held

    def split_copies(owner):
        if owner == holder:
            pairs = [
                (diag_ref.at[1, pl.ds(inner, held), columns], work.at[pl.ds(0, held)]),
                (coup_ref.at[0, pl.ds(inner, PANEL), pl.ds(owner * share, share)], stage),
            ]
            if rest:
                pairs.append((diag_ref.at[1, pl.ds(inner, PANEL), pl.ds(share, share)], turned))
        else:
            pairs = [(other_ref.at[pl.ds(inner, held)], work.at[pl.ds(0, held)])]
            for c in range(0, share, PANEL):
                pairs.append((other_ref.at[pl.ds(share + c, PANEL)], stage.at[:, pl.ds(c, PANEL)]))
            if rest:
                pairs.append((diag_ref.at[1, :, columns], work.at[pl.ds(held, rest)]))
        return [pltpu.make_async_copy(*pair, sems.at[n]) for n, pair in enumerate(pairs)]

    for owner in range(2):
        @pl.when(member == owner)
        def _():
            for copy in split_copies(owner):
                copy.start()

    same = [
        pltpu.make_async_copy(coup_ref.at[1, :, columns], work.at[pl.ds(second_at, share)], sems.at[4]),
        pltpu.make_async_copy(arrow_ref.at[1, :, columns], work.at[pl.ds(third_at, effects)], sems.at[5]),
        pltpu.make_async_copy(
            other_ref.at[pl.ds(nodes + holder * effects, effects)], work.at[pl.ds(third_at + effects, effects)], sems.at[6]
        ),
    ]
    first = []
    for j in range(index):
        skip = start - j * PANEL
        for n, (source, target) in enumerate(((earlier[2 * j], high_before), (earlier[2 * j + 1], low_before))):
            for copies, at, size in ((first, 0, PANEL), (same, PANEL, total - PANEL)):
                sem = before_sems.at[4 * j + 2 * n + (at > 0)]
                copies.append(
                    pltpu.make_async_copy(source.at[pl.ds(skip + at, size)], target.at[j, pl.ds(at, size)], sem)
                )
    for copy in first + same:
        copy.start()
    if start:
        factor[0:start, :] = jnp.zeros((start, PANEL), jnp.float32)
    def update(at, size):
        if not index:
            return
        value = work[at : at + size, :]
        for j in range(index):
            left = left_terms(high_before[j, at : at + size, :], low_before[j, at : at + size, :])
            right = right_terms(high_before[j, 0:PANEL, :], low_before[j, 0:PANEL, :])
            value = value - plain_nt(left, right)
        work[at : at + size, :] = value

    split_copies(0)[0].wait()
    for copy in first:
        copy.wait()
    update(0, PANEL)
    for owner in range(2):
        @pl.when(member == owner)
        def _():
            for copy in split_copies(owner)[1:]:
                copy.wait()
            if owner == holder and rest:
                for r in range(0, PANEL, BLOCK):
                    for c in range(0, rest, BLOCK):
                        work[held + c : held + c + BLOCK, r : r + BLOCK] = turned[r : r + BLOCK, c : c + BLOCK].T

    for copy in same:
        copy.wait()

    @pl.when(open_ref[0] == 0)
    def _():
        work[second_at : second_at + share, :] = jnp.zeros((share, PANEL), jnp.float32)

    for r in range(0, PANEL, BLOCK):
        for c in range(0, share, BLOCK):
            work[first_at + c : first_at + c + BLOCK, r : r + BLOCK] = stage[r : r + BLOCK, c : c + BLOCK].T

    waiting = spans(PANEL, total, BLOCK)
    tasks = [[] for _ in range(32)]
    for n, (at, size) in enumerate(waiting):
        tasks[(32 * n) // len(waiting)].append(functools.partial(update, at, size))

    head = work[0:BLOCK, 0:BLOCK]
    side = work[BLOCK:PANEL, 0:BLOCK]
    tail = work[BLOCK:PANEL, BLOCK:PANEL]
    head_inverse = inverse_of_factor(head, tasks[:16])
    beside = exact(side, head_inverse, 1)
    across = exact(beside, head_inverse, 0)
    tail_inverse = inverse_of_factor(tail - exact(beside, beside, 1), tasks[16:])
    corner = -exact(tail_inverse, across, 0)
    inverse = jnp.concatenate(
        [
            jnp.concatenate([head_inverse, jnp.zeros((BLOCK, BLOCK), jnp.float32)], axis=1),
            jnp.concatenate([corner, tail_inverse], axis=1),
        ],
        axis=0,
    )
    right = right_terms(*split(inverse))

    def solve(at, size):
        solved = plain_nt(left_terms(*split(work[at : at + size, :])), right)
        if at < PANEL:
            row = lax.broadcasted_iota(jnp.int32, solved.shape, 0) + at
            lane = lax.broadcasted_iota(jnp.int32, solved.shape, 1)
            solved = jnp.where(row >= lane, solved, 0.0)
        if at < square:
            factor[start + at : start + at + size, :] = solved
        else:
            work[at : at + size, :] = solved
        high[at : at + size, :], low[at : at + size, :] = split(solved)

    sends = [
        (work.at[pl.ds(second_at, 2 * share + effects)], send_ref),
        (work.at[pl.ds(first_at, share)], cross_ref),
        (work.at[pl.ds(first_at, share)], first_ref.at[0, :, columns]),
        (work.at[pl.ds(second_at, share)], second_ref.at[0, :, columns]),
        (work.at[pl.ds(third_at, effects)], third_ref.at[0, :, columns]),
        (factor.at[pl.ds(pl.multiple_of(member * share, share), share)], factor_ref.at[0, :, columns]),
        (high, high_ref),
        (low, low_ref),
    ]
    sends = [pltpu.make_async_copy(source, target, out_sems.at[n]) for n, (source, target) in enumerate(sends)]
    for at, size in spans(square, total, PANEL):
        solve(at, size)
    for copy in sends[:5]:
        copy.start()
    for at, size in spans(0, square, PANEL):
        solve(at, size)
    for copy in sends[5:]:
        copy.start()
    if last:
        at, size = third_at, 2 * effects
        value = plain_nt(
            left_terms(high[at : at + effects, :], low[at : at + effects, :]),
            right_terms(high[at : at + size, :], low[at : at + size, :]),
        )
        for j in range(index):
            value = value + plain_nt(
                left_terms(high_before[j, at : at + effects, :], low_before[j, at : at + effects, :]),
                right_terms(high_before[j, at : at + size, :], low_before[j, at : at + size, :]),
            )
        crossed = jnp.concatenate([value[:, effects:], value[:, :effects]], axis=1)
        corner_ref[...] = jnp.where(member == 0, value, crossed)
    for copy in sends:
        copy.wait()


def panel(index, inputs, earlier, results, order):
    member, opened, diag_block, coupling, arrow, other = inputs
    share, nodes = diag_block.shape[1:]
    effects = arrow.shape[1]
    count = nodes // PANEL
    total = nodes - index * PANEL + 2 * share + 2 * effects
    anywhere = pl.BlockSpec(memory_space=pl.ANY)
    scalar = pl.BlockSpec(memory_space=pltpu.SMEM)
    pinned = pl.BlockSpec(memory_space=pltpu.HBM)
    whole = pl.BlockSpec(memory_space=pltpu.VMEM)
    shapes = [
        ((1, share, nodes), jnp.float32), ((1, share, nodes), jnp.float32),
        ((1, share, nodes), jnp.float32), ((1, effects, nodes), jnp.float32),
        ((2 * share + effects, PANEL), jnp.float32), ((share, PANEL), jnp.float32),
        ((total, PANEL), jnp.bfloat16), ((total, PANEL), jnp.bfloat16),
    ]
    outs = [anywhere] * len(shapes)
    if index == count - 1:
        shapes.append(((effects, 2 * effects), jnp.float32))
        outs.append(pl.BlockSpec(memory_space=pltpu.VMEM))
    operands = [*inputs, *earlier, *results, *order]
    aliases = {6 + len(earlier) + n: n for n in range(len(results))}
    return pl.pallas_call(
        functools.partial(panel_kernel, index, count, share, effects, len(results) + len(order)),
        out_shape=[jax.ShapeDtypeStruct(shape, kind) for shape, kind in shapes],
        in_specs=[scalar, scalar, *[pinned] * 3, *[anywhere] * (len(operands) - 5)],
        out_specs=outs,
        scratch_shapes=[
            pltpu.VMEM((total, PANEL), jnp.float32),
            pltpu.VMEM((PANEL, share), jnp.float32),
            pltpu.VMEM((PANEL, share), jnp.float32),
            pltpu.VMEM((nodes, PANEL), jnp.float32),
            pltpu.VMEM((total, PANEL), jnp.bfloat16),
            pltpu.VMEM((total, PANEL), jnp.bfloat16),
            pltpu.VMEM((max(index, 1), total, PANEL), jnp.bfloat16),
            pltpu.VMEM((max(index, 1), total, PANEL), jnp.bfloat16),
            pltpu.SemaphoreType.DMA((7,)),
            pltpu.SemaphoreType.DMA((max(4 * index, 1),)),
            pltpu.SemaphoreType.DMA((8,)),
        ],
        input_output_aliases=aliases,
        compiler_params=pltpu.CompilerParams(vmem_limit_bytes=(40 if index else 56) * 1024 * 1024),
        cost_estimate=SMALL,
        name=f"panel_{index}",
    )(*operands)


def exchange_kernel(n, where_ref, diag_ref, coup_ref, arrow_ref, out, sems):
    share, nodes = diag_ref.shape[1:]
    effects = arrow_ref.shape[1]
    member = where_ref[0]
    own_at = pl.multiple_of(member * share, share)
    other_at = pl.multiple_of((1 - member) * share, share)
    pairs = [(diag_ref.at[1, :, pl.ds(own_at + n * PANEL, PANEL)], out.at[pl.ds(0, share)])]
    for c in range(0, share, PANEL):
        pairs.append(
            (coup_ref.at[0, pl.ds(n * PANEL, PANEL), pl.ds(other_at + c, PANEL)], out.at[pl.ds(share + c, PANEL)])
        )
    for m in range(2):
        source = arrow_ref.at[1, :, pl.ds(m * share + n * PANEL, PANEL)]
        pairs.append((source, out.at[pl.ds(nodes + m * effects, effects)]))
    copies = [pltpu.make_async_copy(*pair, sems.at[at]) for at, pair in enumerate(pairs)]
    for copy in copies:
        copy.start()
    for copy in copies:
        copy.wait()


def exchange(n, member, diag_block, coupling, arrow):
    share, nodes = diag_block.shape[1:]
    effects = arrow.shape[1]
    return pl.pallas_call(
        functools.partial(exchange_kernel, n),
        out_shape=jax.ShapeDtypeStruct((nodes + 2 * effects, PANEL), jnp.float32),
        in_specs=[pl.BlockSpec(memory_space=pltpu.SMEM)] + [pl.BlockSpec(memory_space=pltpu.HBM)] * 3,
        out_specs=pl.BlockSpec(memory_space=pltpu.VMEM),
        scratch_shapes=[pltpu.SemaphoreType.DMA((3 + share // PANEL,))],
        compiler_params=pltpu.CompilerParams(vmem_limit_bytes=56 * 1024 * 1024),
        cost_estimate=SMALL,
        name=f"exchange_{n}",
    )(member, diag_block, coupling, arrow)


def own_products_kernel(half, count, share, effects, skipped, *refs):
    where_ref, diag_ref, arrow_ref = refs[:3]
    highs, lows, refs = refs[3 : 3 + count], refs[3 + count : 3 + 2 * count], refs[3 + 2 * count :]
    if half:
        crosses, refs = refs[:count], refs[count:]
    refs = refs[skipped:]
    pivot_ref, right_ref, arrow_out_ref = refs[:3]
    high, low, other, pivot, middle, lines, sems, out_sems = refs[3:]
    member = where_ref[0]
    rows = 2 * share + effects
    columns = pl.ds(pl.multiple_of((1 - member if half else member) * share, share), share)
    copies = []
    for n in range(count):
        skip = highs[n].shape[0] - rows - effects
        copies.append(pltpu.make_async_copy(highs[n].at[pl.ds(skip, rows)], high.at[:, pl.ds(n * PANEL, PANEL)], sems.at[3 * n]))
        copies.append(pltpu.make_async_copy(lows[n].at[pl.ds(skip, rows)], low.at[:, pl.ds(n * PANEL, PANEL)], sems.at[3 * n + 1]))
        if half:
            copies.append(pltpu.make_async_copy(crosses[n], other.at[:, pl.ds(n * PANEL, PANEL)], sems.at[3 * n + 2]))
    copies.append(pltpu.make_async_copy(diag_ref.at[0, :, columns], pivot, sems.at[3 * count]))
    copies.append(pltpu.make_async_copy(arrow_ref.at[0, :, columns], lines, sems.at[3 * count + 1]))
    for copy in copies:
        copy.start()
    for copy in copies:
        copy.wait()
    for c in range(0, share, PANEL):
        if half:
            right = right_terms(*split(other[c : c + PANEL, :]))
        else:
            right = right_terms(high[share + c : share + c + PANEL, :], low[share + c : share + c + PANEL, :])
        for at, size in spans(0, rows, PANEL):
            value = plain_nt(left_terms(high[at : at + size, :], low[at : at + size, :]), right)
            if at < share:
                middle[at : at + size, c : c + PANEL] = -value
            elif at < 2 * share:
                to = at - share
                pivot[to : to + size, c : c + PANEL] = pivot[to : to + size, c : c + PANEL] - value
            else:
                lines[:, c : c + PANEL] = lines[:, c : c + PANEL] - value
    results = [
        (pivot, pivot_ref.at[:, columns]), (middle, right_ref.at[0, :, columns]), (lines, arrow_out_ref.at[:, columns])
    ]
    results = [pltpu.make_async_copy(source, target, out_sems.at[n]) for n, (source, target) in enumerate(results)]
    for copy in results:
        copy.start()
    for copy in results:
        copy.wait()


def own_products(half, member, diag_block, arrow, highs, lows, crosses, before):
    share, nodes = diag_block.shape[1:]
    effects = arrow.shape[1]
    count = len(highs)
    rows = 2 * share + effects
    anywhere = pl.BlockSpec(memory_space=pl.ANY)
    scalar = pl.BlockSpec(memory_space=pltpu.SMEM)
    shapes = [(share, nodes), (1, share, nodes), (effects, nodes)]
    operands = [member, diag_block, arrow, *highs, *lows, *crosses]
    aliases = {len(operands) + n: n for n in range(len(before))}
    operands += before
    return pl.pallas_call(
        functools.partial(own_products_kernel, half, count, share, effects, len(before)),
        out_shape=[jax.ShapeDtypeStruct(shape, jnp.float32) for shape in shapes],
        in_specs=[scalar] + [pl.BlockSpec(memory_space=pltpu.HBM)] * 2 + [anywhere] * (len(operands) - 3),
        out_specs=[anywhere] * 3,
        scratch_shapes=[
            pltpu.VMEM((rows, nodes), jnp.bfloat16),
            pltpu.VMEM((rows, nodes), jnp.bfloat16),
            pltpu.VMEM((share, nodes), jnp.float32),
            pltpu.VMEM((share, share), jnp.float32),
            pltpu.VMEM((share, share), jnp.float32),
            pltpu.VMEM((effects, share), jnp.float32),
            pltpu.SemaphoreType.DMA((3 * count + 2,)),
            pltpu.SemaphoreType.DMA((3,)),
        ],
        input_output_aliases=aliases,
        compiler_params=pltpu.CompilerParams(vmem_limit_bytes=40 * 1024 * 1024),
        cost_estimate=SMALL,
        name=f"own_products_{half}",
    )(*operands)


def next_products_kernel(count, with_left, share, effects, *refs):
    where_ref, pivot_in, arrow_in = refs[:3]
    refs = refs[3:]
    if with_left:
        left_in, refs = refs[0], refs[1:]
    owns, others, refs = refs[:count], refs[count : 2 * count], refs[2 * count :]
    pivot_ref, left_ref, arrow_ref, pivot, middle, lines, sems = refs
    member = where_ref[0]
    rows = 2 * share + effects
    own_at = pl.multiple_of(member * share, share)
    other_at = pl.multiple_of((1 - member) * share, share)

    def across(parts, at, size):
        return split(jnp.concatenate([part[at : at + size, :] for part in parts], axis=1))

    right = [[right_terms(*across(parts, c, PANEL)) for c in range(0, share, PANEL)] for parts in (owns, others)]
    copies = []
    for at, size in spans(0, rows, PANEL):
        left = left_terms(*across(owns, at, size))
        to = at % share
        for half, base in ((0, own_at), (1, other_at)):
            for c in range(0, share, PANEL):
                columns = pl.ds(pl.multiple_of(base + c, PANEL), PANEL)
                value = plain_nt(left, right[half][c // PANEL])
                if at < share:
                    pivot[to : to + size, columns] = pivot_in[to : to + size, columns] - value
                elif at >= 2 * share:
                    lines[:, columns] = arrow_in[:, columns] - value
                elif with_left:
                    middle[to : to + size, columns] = left_in[to : to + size, columns] - value
                else:
                    middle[to : to + size, columns] = -value
        source, target = ((pivot, pivot_ref), (middle, left_ref), (lines, arrow_ref))[at // share]
        rows_here = pl.ds(to, size)
        copies.append(pltpu.make_async_copy(source.at[rows_here], target.at[rows_here], sems.at[len(copies)]))
        copies[-1].start()
    for copy in copies:
        copy.wait()


def next_products(member, pivot, arrow, left, owns, others):
    share, nodes = pivot.shape
    effects = arrow.shape[0]
    count = len(owns)
    rows = 2 * share + effects
    anywhere = pl.BlockSpec(memory_space=pl.ANY)
    scalar = pl.BlockSpec(memory_space=pltpu.SMEM)
    with_left = left is not None
    operands = [member, pivot, arrow] + ([left] if with_left else []) + [*owns, *others]
    shapes = [(share, nodes), (share, nodes), (effects, nodes)]
    return pl.pallas_call(
        functools.partial(next_products_kernel, count, with_left, share, effects),
        out_shape=[jax.ShapeDtypeStruct(shape, jnp.float32) for shape in shapes],
        in_specs=[scalar] + [pl.BlockSpec(memory_space=pltpu.VMEM)] * (len(operands) - 1),
        out_specs=[anywhere] * 3,
        scratch_shapes=[
            pltpu.VMEM((share, nodes), jnp.float32),
            pltpu.VMEM((share, nodes), jnp.float32),
            pltpu.VMEM((effects, nodes), jnp.float32),
            pltpu.SemaphoreType.DMA((len(spans(0, rows, PANEL)),)),
        ],
        compiler_params=pltpu.CompilerParams(vmem_limit_bytes=28 * 1024 * 1024),
        cost_estimate=SMALL,
        name=f"next_products_{count}",
    )(*operands)


def local(diag_block, coupling, arrow, corner):
    partition_count = lax.axis_size("tm")
    position = lax.axis_index("tm")
    at = lax.axis_index("blk").astype(jnp.int32)
    member = at.reshape((1,))
    opened = (position < partition_count - 1).astype(jnp.int32).reshape((1,))
    share, nodes = diag_block.shape[1:]
    halves = [swapped(exchange(n, member, diag_block, coupling, arrow)) for n in range(share // PANEL)]
    earlier, results, highs, lows, crosses, owns, others = [], [], [], [], [], [], []
    for index in range(nodes // PANEL):
        inputs = (member, opened, diag_block, coupling, arrow, halves[index % len(halves)])
        order = []
        if index > 1:
            order = [*owns[index - 3 : index - 2], crosses[index - 2]]
        found = panel(index, inputs, earlier, results, order)
        results = found[:4]
        send, cross, high, low = found[4:8]
        earlier += [high, low]
        highs.append(high)
        lows.append(low)
        if index == nodes // PANEL - 1:
            sums = corner_rounds(partition_count)
            total = found[8] if sums else lax.psum(found[8], "tm")
            for steps, size in sums[:-1]:
                total = grouped_sum(total, "tm", steps, size)
            send = after(send, total)
        owns.append(shifted(send, "tm", 1))
        crosses.append(swapped(cross))
        if index < nodes // PANEL - 2:
            others.append(swapped(owns[-1][:share]))
    products = own_products(0, after(member, *owns[1:-2]), diag_block, arrow, highs, lows, [], [])
    products = own_products(1, member, diag_block, arrow, highs, lows, crosses, products)
    pivot, right_out, lines = products
    before = after(owns[-2], products[0])
    others.append(swapped(before[:share]))
    pivot, left, lines = next_products(member, pivot, lines, None, [*owns[:-2], before], others)
    final = after(owns[-1], pivot)
    pivot, left, lines = next_products(member, pivot, lines, left, [final], [swapped(final[:share])])
    for steps, size in sums[-1:]:
        total = grouped_sum(total, "tm", steps, size, pivot)
    corner_out = corner - total
    return (*results, pivot[None], left[None], right_out, lines[None], corner_out)


def solution(mesh):
    placed = (P("tm", "blk", None), P("tm", "blk", None), P("tm", "blk", None), P("blk", None))
    return jax.shard_map(
        local,
        mesh=mesh,
        in_specs=placed,
        out_specs=(P("tm", "blk", None),) * 8 + (P("blk", None),),
        check_vma=False,
    )
```
